128 devices in a mesh: gx: 16 (over y, z), gy: 8 (over x, core).
Axes of the slice: x: 4, y: 4, z: 4, core: 2. Of those that a mesh axis runs over, the one named last changes fastest.
Arguments:
- particle_feat: bfloat16 [2048, 64, 128], P(('gx', 'gy')), may hold values from -6 to 6
- block_counts: int32 [2048], P(('gx', 'gy')), may hold values from 1 to 128, 196608 in all
- entry_block: int32 [4096], P(('gx', 'gy')), may hold values from 0 to 15
- entry_dest: int32 [4096, 1], P(('gx', 'gy')), may hold values from 0 to 127, as said below
- entry_nodes: int32 [4096, 128], P(('gx', 'gy')), may hold values from 0 to 4095
- entry_weights: bfloat16 [4096, 128, 128], P(('gx', 'gy')), may hold values from 0 to 0.1796875
- conv_in: bfloat16 [3, 64, 576], replicated, may hold values from -0.15625 to 0.15625
- conv_mid: bfloat16 [3, 64, 576], replicated, may hold values from -0.15625 to 0.15625
- conv_out: bfloat16 [3, 64, 576], replicated, may hold values from -0.15625 to 0.15625
- head_weight: float32 [3, 64], replicated, may hold values from -0.75 to 0.75
Outputs:
- velocity: float32 [2048, 3, 128], P(('gx', 'gy'))
The draws below stay inside these ranges and needn't reach their ends.
Inputs may be any that keep to these rules, and one draw needn't show every extreme that they name: `entry_dest`: linear index 8 * (x index) + (y index) of the tile; it is the sending device's own tile or a tile beside it in x, y or both (one step each way, no wrap); among the rows of one device no tile is named more than 8 times, and the sender's own tile exactly 8 times. `block_counts`: the first that many slots of the block are live; some block is full.
All inputs are finite; a program needn't handle non-finite values.
Results may differ from the reference program's by a relative error of at most 0.0045.
Values may be sent and summed in bfloat16 or wider, within the bound.
No kernel may reach another device: no remote copies, remote signals or barrier semaphores. Data moves between devices by JAX's collectives and lax.ppermute only.
A program may use at most 128 MiB of HBM per device.

```python
import math
import jax
import jax.numpy as jnp
import numpy as np
from jax import lax

CHAN = 64
PART = 128
NODES = 128
BLOCK_DEV = 16
TILE_X = 4
TILE_Y = 8
TILE_Z = 128
ENTRY_DEV = 32
CAPACITY = 8
CELLS = 4096
ENTRIES = 4096
BLOCKS = 2048
NX = 64
NY = 64
NZ = 128
N_GX = 16
N_GY = 8


def draw_entry_dest(key, part):
    key = jax.random.fold_in(key, 11)
    score_key, order_key = jax.random.split(key)
    owners = N_GX * N_GY
    slot_count = 9 * CAPACITY
    slot = jnp.arange(slot_count, dtype=jnp.int32)
    direction = slot // CAPACITY
    step_x = direction // 3 - 1
    step_y = direction % 3 - 1
    device = jnp.arange(owners, dtype=jnp.int32)
    tile_x = device[:, None] // N_GY + step_x[None, :]
    tile_y = device[:, None] % N_GY + step_y[None, :]
    valid = (tile_x >= 0) & (tile_x < N_GX) & (tile_y >= 0) & (tile_y < N_GY)
    base = jax.random.randint(score_key, (owners, slot_count), 0, 65536)
    score = base * slot_count + slot[None, :]
    score = jnp.where(valid, score, -1 - slot[None, :])
    score = jnp.where(direction[None, :] == 4, 1073741824 + slot[None, :], score)
    picked_scores, picked = lax.top_k(score, ENTRY_DEV)
    linear = jnp.clip(tile_x, 0, N_GX - 1) * N_GY + jnp.clip(tile_y, 0, N_GY - 1)
    chosen = jnp.take_along_axis(linear, picked, axis=1)
    row_keys = jax.random.split(order_key, owners)
    shuffled = jax.vmap(lambda k, row: row[jax.random.permutation(k, ENTRY_DEV)])(row_keys, chosen)
    return shuffled.reshape(ENTRIES, 1).astype(jnp.int32)


def set_ends(entries, key, smallest, top_value):
    extent = entries.shape
    spot = [jax.random.randint(jax.random.fold_in(key, axis), (), 0, extent[axis]) for axis in range(len(extent))]
    entries = entries.at[tuple(spot)].set(smallest)
    longest = extent.index(max(extent))
    spot[longest] = (spot[longest] + 1) % extent[longest]
    return entries.at[tuple(spot)].set(top_value)


def block_levels(own_key, dims, cuts, least, top_value):
    gain, own = 1.0, jax.random.fold_in(own_key, 6)
    for dim, parts in cuts:
        draws = jnp.exp(jax.random.uniform(jax.random.fold_in(own, dim), (parts,), jnp.float32, least / len(cuts), top_value / len(cuts)))
        gain = gain * jnp.repeat(draws, dims[dim] // parts).reshape([-1 if axis == dim else 1 for axis in range(len(dims))])
    return gain


def profile(count, total, bound, slope):
    loads = [(1 << 20) // math.isqrt(standing ** slope) + 1 for standing in range(2, count + 1)]
    spare, given = total - bound - (count - 1), [1] * (count - 1)
    while spare > 0:
        candidates = [i for i in range(count - 1) if given[i] < bound]
        whole, remaining = sum([loads[i] for i in candidates]), spare
        for i in candidates:
            more = min(bound - given[i], max(1, remaining * loads[i] // whole), spare)
            given[i] = given[i] + more
            spare = spare - more
    return np.array([bound] + given)


def ragged(own_key, amount, total, most, skew):
    if amount == 2:
        one = jax.random.randint(own_key, (), max(1, total - most), min(most, total - 1) + 1)
        return jnp.stack([one, total - one])
    sizes = jnp.asarray(profile(amount, total, most, skew), jnp.int32)
    pairs = (amount - 1) // 2
    giver, taker = sizes[1:1 + 2 * pairs:2], sizes[2:2 + 2 * pairs:2]
    margin = jnp.minimum(giver - 1, most - taker)
    shifted = jax.random.randint(jax.random.fold_in(own_key, 1), (pairs,), 0, 1 << 20) % (margin + 1)
    sizes = sizes.at[1:1 + 2 * pairs:2].set(giver - shifted).at[2:2 + 2 * pairs:2].set(taker + shifted)
    return sizes[jax.random.permutation(jax.random.fold_in(own_key, 2), amount)]


def scatter_about(rng, extent, width, limit, pieces=(), kind=jnp.bfloat16):
    gain = block_levels(rng, extent, pieces, -0.22, 0.18) if pieces else 1.0
    array = jax.random.normal(rng, extent, jnp.float32) * width * gain
    return jnp.minimum(jnp.maximum(array, -limit), limit).astype(kind)


def setup_inputs(seed: int = 0) -> dict:
    key_list = jax.random.split(jax.random.key(seed), 11)
    particle_feat = scatter_about(key_list[0], (BLOCKS, CHAN, PART), 1.0, 6.0, ((0, 128),))
    block_counts = ragged(key_list[1], BLOCKS, BLOCKS * PART * 3 // 4, PART, 1).astype(jnp.int32)
    entry_block = set_ends(jax.random.randint(key_list[2], (ENTRIES,), 0, BLOCK_DEV), jax.random.fold_in(key_list[2], 1), 0, BLOCK_DEV - 1).astype(jnp.int32)
    entry_dest = draw_entry_dest(jax.random.fold_in(key_list[10], 71), 0)
    entry_nodes = set_ends(jax.random.randint(key_list[4], (ENTRIES, NODES), 0, CELLS), jax.random.fold_in(key_list[4], 1), 0, CELLS - 1).astype(jnp.int32)
    entry_weights = jnp.clip(0.1796875 * jax.random.uniform(key_list[5], (ENTRIES, PART, NODES), jnp.float32) ** block_levels(key_list[5], (ENTRIES, PART, NODES), ((0, 128),), -0.2, 0.2), 0.0, 0.1796875).astype(jnp.bfloat16)
    conv_in = scatter_about(key_list[6], (3, CHAN, 9 * CHAN), (27 * CHAN) ** -0.5, 0.15625)
    conv_mid = scatter_about(key_list[7], (3, CHAN, 9 * CHAN), (27 * CHAN) ** -0.5, 0.15625)
    conv_out = scatter_about(key_list[8], (3, CHAN, 9 * CHAN), (27 * CHAN) ** -0.5, 0.15625)
    head_weight = scatter_about(key_list[9], (3, CHAN), CHAN ** -0.5, 0.75, (), jnp.float32)
    return {"particle_feat": particle_feat, "block_counts": block_counts, "entry_block": entry_block, "entry_dest": entry_dest, "entry_nodes": entry_nodes, "entry_weights": entry_weights, "conv_in": conv_in, "conv_mid": conv_mid, "conv_out": conv_out, "head_weight": head_weight}


def conv(volume, weight):
    chans, size_x, size_y, size_z = volume.shape
    padded = jnp.pad(volume, ((0, 0), (1, 1), (1, 1), (1, 1)))
    result = jnp.zeros((chans, size_x * size_y * size_z), jnp.float32)
    for shift_a in range(3):
        for shift_b in range(3):
            for shift_c in range(3):
                start = (3 * shift_b + shift_c) * chans
                tap = weight[shift_a][:, start:start + chans].astype(jnp.float32)
                window = padded[:, shift_a:shift_a + size_x, shift_b:shift_b + size_y, shift_c:shift_c + size_z]
                result = result + jnp.dot(tap, window.reshape(chans, -1).astype(jnp.float32))
    return result.reshape(chans, size_x, size_y, size_z)


def reference(particle_feat, block_counts, entry_block, entry_dest, entry_nodes, entry_weights, conv_in, conv_mid, conv_out, head_weight):
    slots = jnp.arange(PART, dtype=jnp.int32)
    live = (slots[None, :] < block_counts[:, None]).astype(jnp.float32)
    masked = particle_feat.astype(jnp.float32) * live[:, None, :]
    owner = jnp.arange(ENTRIES, dtype=jnp.int32) // ENTRY_DEV
    global_block = (owner * BLOCK_DEV + entry_block).astype(jnp.int32)
    partial_value = jnp.einsum("ecp,epk->eck", masked[global_block], entry_weights.astype(jnp.float32)).astype(jnp.bfloat16)
    target = entry_dest[:, 0]
    tile_x = target // N_GY
    tile_y = target % N_GY
    local_x = entry_nodes // (TILE_Y * TILE_Z)
    local_y = entry_nodes // TILE_Z % TILE_Y
    local_z = entry_nodes % TILE_Z
    flat = ((tile_x[:, None] * TILE_X + local_x) * NY + tile_y[:, None] * TILE_Y + local_y) * NZ + local_z
    flat = flat.astype(jnp.int32)
    spread = jnp.transpose(partial_value.astype(jnp.float32), (1, 0, 2)).reshape(CHAN, -1)
    grid = jnp.zeros((CHAN, NX * NY * NZ), jnp.float32).at[:, flat.reshape(-1)].add(spread)
    grid = grid.reshape(CHAN, NX, NY, NZ).astype(jnp.bfloat16)
    act = (jax.nn.silu(conv(grid, conv_in)) + grid.astype(jnp.float32)).astype(jnp.bfloat16)
    coarse = (act.astype(jnp.float32).reshape(CHAN, NX // 2, 2, NY // 2, 2, NZ).sum(axis=(2, 4)) * 0.25).astype(jnp.bfloat16)
    mid = jax.nn.silu(conv(coarse, conv_mid)).astype(jnp.bfloat16)
    raised = jnp.repeat(jnp.repeat(mid, 2, axis=1), 2, axis=2)
    merged = (act.astype(jnp.float32) + raised.astype(jnp.float32)).astype(jnp.bfloat16)
    field = conv(merged, conv_out).astype(jnp.bfloat16)
    sampled = field.reshape(CHAN, -1)[:, flat.reshape(-1)].reshape(CHAN, ENTRIES, NODES)
    back = jnp.einsum("cek,epk->ecp", sampled.astype(jnp.float32), entry_weights.astype(jnp.float32))
    particle_vals = jax.ops.segment_sum(back, global_block, BLOCKS)
    velocity = jnp.einsum("dc,bcp->bdp", head_weight, particle_vals, precision=lax.Precision.HIGHEST)
    return velocity * live[:, None, :]
```

```python
import functools

import jax
import jax.numpy as jnp
from jax import lax
from jax.experimental import pallas as pl
from jax.experimental.pallas import tpu as pltpu
from jax.sharding import PartitionSpec as P

BF = jnp.bfloat16
F32 = jnp.float32
I32 = jnp.int32

CHAN = 64
LANES = 128
TILE_X = 4
TILE_Y = 8
SLOTS = 8
GROUP = 4
VMEM_LIMIT = 40 * 1024 * 1024

VM = pl.BlockSpec(memory_space=pltpu.VMEM)
SM = pl.BlockSpec(memory_space=pltpu.SMEM)
NT = (((1,), (1,)), ((), ()))


def call(kernel, outs, ins, scratch, flops):
    return pl.pallas_call(
        kernel,
        out_shape=[jax.ShapeDtypeStruct(s, d) for s, d in outs],
        in_specs=ins,
        out_specs=[VM] * len(outs),
        scratch_shapes=scratch,
        compiler_params=pltpu.CompilerParams(vmem_limit_bytes=VMEM_LIMIT),
        cost_estimate=pl.CostEstimate(flops=flops, bytes_accessed=2000000, transcendentals=0),
    )


def partial_kernel(
    where_ref, counts_ref, block_ref, dest_ref, feat_ref, nodes_ref, weight_ref, *rest
):
    outs = rest[:9]
    part, hi_all, lo_all, index, taken, entry_of = rest[9:]
    entries = weight_ref.shape[0]
    lane = lax.broadcasted_iota(I32, (CHAN, LANES), 1)
    for e in range(entries):
        block = block_ref[e]
        feat = jnp.where(lane < counts_ref[block], feat_ref[block].astype(F32), 0.0).astype(BF)
        value = jnp.dot(feat, weight_ref[e], preferred_element_type=F32)
        part[e] = value.astype(BF)
    nodes = nodes_ref[...]
    hi_all[...] = (nodes >> 8).astype(F32)
    lo_all[...] = (nodes & 255).astype(F32)
    index[...] = jnp.full(index.shape, -1.0, F32)
    for d in range(9):
        taken[d] = 0

    def place(e, carry):
        tile = dest_ref[e]
        d = (tile // where_ref[2] - where_ref[0] + 1) * 3 + (tile % where_ref[2] - where_ref[1] + 1)
        s = taken[d]
        taken[d] = s + 1
        entry_of[d * SLOTS + s] = e
        index[pl.ds(d * 16 + s, 1), :] = hi_all[pl.ds(e, 1), :]
        index[pl.ds(d * 16 + 8 + s, 1), :] = lo_all[pl.ds(e, 1), :]
        return carry

    lax.fori_loop(0, entries, place, 0)
    for d in range(9):
        count = taken[d]

        def copy(s, carry, d=d):
            outs[d][s] = part[entry_of[d * SLOTS + s]]
            return carry

        lax.fori_loop(0, count, copy, 0)
        outs[d][SLOTS, 0:16, :] = index[d * 16 : d * 16 + 16, :].astype(BF)
        outs[d][SLOTS, 16:32, :] = jnp.full((16, LANES), count.astype(F32), F32).astype(BF)
        outs[d][SLOTS, 32:64, :] = jnp.zeros((32, LANES), BF)


def scatter_kernel(*refs):
    got = refs[:9]
    grid_ref, low_ref, high_ref = refs[9:12]
    values, index, hi_all, lo_all, acc = refs[12:]
    hi_all[...] = jnp.full(hi_all.shape, -1.0, F32)
    lo_all[...] = jnp.full(lo_all.shape, -1.0, F32)
    acc[...] = jnp.zeros(acc.shape, F32)
    counts = []
    for d in range(9):
        index[d * 16 : d * 16 + 16, :] = got[d][SLOTS, 0:16, :].astype(F32)
        counts.append(jnp.max(got[d][SLOTS, 16:32, :].astype(F32)).astype(I32))
    filled = jnp.int32(0)
    for d in range(9):

        def copy(s, pos, d=d):
            values[pos] = got[d][s]
            hi_all[pl.ds(pos, 1), :] = index[pl.ds(d * 16 + s, 1), :]
            lo_all[pl.ds(pos, 1), :] = index[pl.ds(d * 16 + 8 + s, 1), :]
            return pos + 1

        filled = lax.fori_loop(0, counts[d], copy, filled)
    row = lax.broadcasted_iota(I32, (256, LANES), 0).astype(F32)

    def step(g, carry):
        left = [[] for _ in range(16)]
        right = []
        for j in range(GROUP):
            e = g * GROUP + j
            value = values[e]
            hi = jnp.broadcast_to(hi_all[pl.ds(e, 1), :], (CHAN, LANES)).astype(BF)
            lo = lo_all[pl.ds(e, 1), :]
            right.append(jnp.where(row == lo, 1.0, 0.0).astype(BF))
            for t in range(16):
                left[t].append(jnp.where(hi == jnp.array(t, BF), value, jnp.array(0, BF)))
        a = jnp.concatenate([jnp.concatenate(rows, axis=1) for rows in left], axis=0)
        b = jnp.concatenate(right, axis=1)
        acc[...] += lax.dot_general(a, b, NT, preferred_element_type=F32)
        return carry

    lax.fori_loop(0, (filled + GROUP - 1) // GROUP, step, 0)
    for t in range(16):
        for half in range(2):
            column = acc[t * CHAN : (t + 1) * CHAN, half * LANES : (half + 1) * LANES].astype(BF)
            x = t // 4
            y = (t % 4) * 2 + half
            grid_ref[x, y] = column
            if x == 0:
                low_ref[y] = column
            if x == TILE_X - 1:
                high_ref[y] = column


def shifted(column):
    lane = lax.broadcasted_iota(I32, column.shape, 1)
    wide = column.astype(F32)
    before = jnp.where(lane == 0, 0.0, pltpu.roll(wide, 1, 1)).astype(BF)
    after = jnp.where(lane == LANES - 1, 0.0, pltpu.roll(wide, LANES - 1, 1)).astype(BF)
    return jnp.concatenate([before, column, after], axis=0)


def conv_rows(stack, weight_ref, size_x, size_y, put):
    weight = weight_ref[...]
    for y in range(0, size_y, 2):
        sums = [None] * size_x
        for x in range(size_x + 2):
            rhs = jnp.concatenate(
                [
                    stack[x, y : y + 3].reshape(9 * CHAN, LANES),
                    stack[x, y + 1 : y + 4].reshape(9 * CHAN, LANES),
                ],
                axis=1,
            )
            first = max(0, x - size_x + 1)
            last = min(2, x)
            prod = jnp.dot(
                weight[first * CHAN : (last + 1) * CHAN], rhs, preferred_element_type=F32
            )
            for a in range(first, last + 1):
                piece = prod[(a - first) * CHAN : (a - first + 1) * CHAN]
                out = x - a
                sums[out] = piece if sums[out] is None else sums[out] + piece
            if x >= 2:
                put(x - 2, y, sums[x - 2][:, :LANES])
                put(x - 2, y + 1, sums[x - 2][:, LANES:])
                sums[x - 2] = None


def silu(v):
    return v / (1.0 + jnp.exp(-v))


def edges(where_ref):
    x_lo = where_ref[0] > 0
    x_hi = where_ref[0] < where_ref[3] - 1
    y_lo = where_ref[1] > 0
    y_hi = where_ref[1] < where_ref[2] - 1
    return x_lo, x_hi, y_lo, y_hi


def masked(column, *conditions):
    keep = functools.reduce(jnp.logical_and, conditions)
    return jnp.where(keep, column.astype(F32), 0.0).astype(BF)


def first_conv_kernel(
    where_ref, grid_ref, xl_ref, xh_ref, yl_ref, yh_ref, weight_ref,
    act_ref, coarse_ref, low_ref, high_ref, stack,
):
    x_lo, x_hi, y_lo, y_hi = edges(where_ref)
    for x in range(TILE_X):
        for y in range(TILE_Y):
            stack[x + 1, y + 1] = shifted(grid_ref[x, y])
    for y in range(TILE_Y):
        stack[0, y + 1] = shifted(masked(xl_ref[y], x_lo))
        stack[TILE_X + 1, y + 1] = shifted(masked(xh_ref[y], x_hi))
    for x in range(TILE_X + 2):
        more = (x_lo,) if x == 0 else (x_hi,) if x == TILE_X + 1 else ()
        stack[x, 0] = shifted(masked(yl_ref[x], y_lo, *more))
        stack[x, TILE_Y + 1] = shifted(masked(yh_ref[x], y_hi, *more))

    def put(x, y, value):
        result = (silu(value) + grid_ref[x, y].astype(F32)).astype(BF)
        act_ref[x, y] = result
        if x == 0:
            low_ref[y] = result
        if x == TILE_X - 1:
            high_ref[y] = result

    conv_rows(stack, weight_ref, TILE_X, TILE_Y, put)
    for x in range(TILE_X // 2):
        for y in range(TILE_Y // 2):
            total = (
                act_ref[2 * x, 2 * y].astype(F32)
                + act_ref[2 * x, 2 * y + 1].astype(F32)
                + act_ref[2 * x + 1, 2 * y].astype(F32)
                + act_ref[2 * x + 1, 2 * y + 1].astype(F32)
            )
            result = (total * 0.25).astype(BF)
            coarse_ref[x, y] = result
            low_ref[TILE_Y + x * 4 + y] = result
            high_ref[TILE_Y + x * 4 + y] = result


def second_conv_kernel(
    where_ref, act_ref, coarse_ref, xl_ref, xh_ref, yl_ref, yh_ref, mid_weight_ref, out_weight_ref,
    field_ref, stack, merged, mid_ref, taps,
):
    x_lo, x_hi, y_lo, y_hi = edges(where_ref)
    half_x = TILE_X // 2
    half_y = TILE_Y // 2
    for x in range(half_x):
        for y in range(half_y):
            stack[x + 2, y + 2] = shifted(coarse_ref[x, y])
            stack[x, y + 2] = shifted(masked(xl_ref[TILE_Y + x * half_y + y], x_lo))
            stack[x + 2 + half_x, y + 2] = shifted(
                masked(xh_ref[TILE_Y + x * half_y + y], x_hi)
            )
    for x in range(half_x + 4):
        more = (x_lo,) if x < 2 else (x_hi,) if x >= half_x + 2 else ()
        for y in range(2):
            stack[x, y] = shifted(masked(yl_ref[TILE_X + 2 + x * 2 + y], y_lo, *more))
            stack[x, half_y + 2 + y] = shifted(
                masked(yh_ref[TILE_X + 2 + x * 2 + y], y_hi, *more)
            )

    def put(x, y, value):
        mid_ref[x, y] = silu(value).astype(BF)

    conv_rows(stack, mid_weight_ref, half_x + 2, half_y + 2, put)
    for x in range(TILE_X + 2):
        for y in range(TILE_Y + 2):
            more = ()
            if x == 0:
                more += (x_lo,)
            if x == TILE_X + 1:
                more += (x_hi,)
            if y == 0:
                fine = yl_ref[x]
                more += (y_lo,)
            elif y == TILE_Y + 1:
                fine = yh_ref[x]
                more += (y_hi,)
            elif x == 0:
                fine = xl_ref[y - 1]
            elif x == TILE_X + 1:
                fine = xh_ref[y - 1]
            else:
                fine = act_ref[x - 1, y - 1]
            value = fine.astype(F32) + mid_ref[(x + 1) // 2, (y + 1) // 2].astype(F32)
            if more:
                value = jnp.where(functools.reduce(jnp.logical_and, more), value, 0.0)
            merged[x, y] = value.astype(BF)
    weight = out_weight_ref[...]
    for x in range(TILE_X + 2):
        for y in range(0, TILE_Y + 2, 2):
            pair = jnp.concatenate([merged[x, y], merged[x, y + 1]], axis=1)
            prod = jnp.dot(weight, pair, preferred_element_type=F32)
            taps[x, y] = prod[:, :LANES]
            taps[x, y + 1] = prod[:, LANES:]
    lane = lax.broadcasted_iota(I32, (8, LANES), 1)
    for x in range(TILE_X):
        for y in range(TILE_Y):
            total = None
            for a in range(3):
                for b in range(3):
                    start = (a * 3 + b) * 24
                    piece = taps[x + a, y + b, start : start + 24, :]
                    total = piece if total is None else total + piece
            before = jnp.where(lane == 0, 0.0, pltpu.roll(total[0:8], 1, 1))
            after = jnp.where(lane == LANES - 1, 0.0, pltpu.roll(total[16:24], LANES - 1, 1))
            both = before + total[8:16] + after
            both = both[0:3] + both[3:6]
            for d in range(3):
                field_ref[d, x * TILE_Y + y : x * TILE_Y + y + 1, :] = both[d : d + 1]


def gather_kernel(
    where_ref, counts_ref, block_ref, dest_ref, own_ref, xl_ref, xh_ref, yl_ref, yh_ref,
    nodes_ref, weight_ref, out_ref, frame, total,
):
    entries = weight_ref.shape[0]
    blocks = out_ref.shape[0]
    frame[1] = yl_ref[0]
    frame[4] = yl_ref[1]
    frame[7] = yl_ref[2]
    frame[2] = xl_ref[...]
    frame[5] = own_ref[...]
    frame[8] = xh_ref[...]
    frame[3] = yh_ref[0]
    frame[6] = yh_ref[1]
    frame[9] = yh_ref[2]
    total[...] = jnp.zeros(total.shape, F32)
    sub = lax.broadcasted_iota(I32, (8, LANES), 0)
    for e in range(entries):
        tile = dest_ref[e]
        d = (tile // where_ref[2] - where_ref[0] + 1) * 3 + (tile % where_ref[2] - where_ref[1] + 1)
        node = jnp.broadcast_to(nodes_ref[e : e + 1, :], (8, LANES))
        z = node & (LANES - 1)
        column = node >> 7
        rows = []
        for c in range(3):
            picked = None
            for q in range(4):
                table = frame[d + 1, c, q * 8 : q * 8 + 8, :]
                value = jnp.take_along_axis(table, z, axis=1)
                value = jnp.where(column == sub + q * 8, value, 0.0)
                picked = value if picked is None else picked + value
            rows.append(picked)
        wide = jnp.concatenate(rows, axis=0)
        high = wide.astype(BF)
        low = (wide - high.astype(F32)).astype(BF)
        both = jnp.concatenate([high, low], axis=0)
        value = lax.dot_general(both, weight_ref[e], NT, preferred_element_type=F32)
        block = block_ref[e]
        total[block] += value[0:24] + value[24:48]
    lane = lax.broadcasted_iota(I32, (1, LANES), 1)
    for b in range(blocks):
        live = lane < counts_ref[b]
        for c in range(3):
            value = jnp.sum(total[b, c * 8 : c * 8 + 8, :], axis=0, keepdims=True)
            out_ref[b, c : c + 1, :] = jnp.where(live, value, 0.0)


def moved(value, step_x, step_y):
    size_x = lax.axis_size("gx")
    size_y = lax.axis_size("gy")
    pairs = [
        (x * size_y + y, (x + step_x) % size_x * size_y + (y + step_y) % size_y)
        for x in range(size_x)
        for y in range(size_y)
    ]
    return lax.ppermute(value, ("gx", "gy"), pairs)


def shards(
    particle_feat, block_counts, entry_block, entry_dest, entry_nodes, entry_weights,
    conv_in, conv_mid, conv_out, head_weight,
):
    size_x = lax.axis_size("gx")
    size_y = lax.axis_size("gy")
    where = jnp.stack(
        [
            lax.axis_index("gx").astype(I32),
            lax.axis_index("gy").astype(I32),
            jnp.int32(size_y),
            jnp.int32(size_x),
        ]
    )
    blocks = particle_feat.shape[0]
    entries = entry_weights.shape[0]
    dest = entry_dest.reshape(entries)
    in_weight = conv_in.reshape(3 * CHAN, 9 * CHAN)
    mid_weight = conv_mid.reshape(3 * CHAN, 9 * CHAN)
    folded = jnp.einsum(
        "do,aox->adx", head_weight, conv_out.astype(F32), precision=lax.Precision.HIGHEST
    )
    high = lax.reduce_precision(folded, 8, 7)
    both = jnp.concatenate([high, folded - high, jnp.zeros((3, 2, 9 * CHAN), F32)], axis=1)
    out_weight = (
        both.reshape(3, 8, 9, CHAN).transpose(0, 2, 1, 3).reshape(27 * 8, CHAN).astype(BF)
    )

    packed = (SLOTS + 1, CHAN, LANES)
    sent = call(
        partial_kernel,
        [(packed, BF)] * 9,
        [SM] * 4 + [VM] * 3,
        [
            pltpu.VMEM((entries, CHAN, LANES), BF),
            pltpu.VMEM((entries, LANES), F32),
            pltpu.VMEM((entries, LANES), F32),
            pltpu.VMEM((9 * 16, LANES), F32),
            pltpu.SMEM((9,), I32),
            pltpu.SMEM((9 * SLOTS,), I32),
        ],
        70000000,
    )(where, block_counts, entry_block, dest, particle_feat, entry_nodes, entry_weights)
    got = [None] * 9
    got[4] = sent[4]
    for d in (7, 1, 5, 3, 8, 0, 6, 2):
        got[d] = moved(sent[d], d // 3 - 1, d % 3 - 1)
    most = 9 * SLOTS + GROUP
    grid, grid_low, grid_high = call(
        scatter_kernel,
        [((TILE_X, TILE_Y, CHAN, LANES), BF)] + [((TILE_Y, CHAN, LANES), BF)] * 2,
        [VM] * 9,
        [
            pltpu.VMEM((most, CHAN, LANES), BF),
            pltpu.VMEM((9 * 16, LANES), F32),
            pltpu.VMEM((most, LANES), F32),
            pltpu.VMEM((most, LANES), F32),
            pltpu.VMEM((16 * CHAN, 256), F32),
        ],
        2400000000,
    )(*got)

    xl = moved(grid_high, 1, 0)
    xh = moved(grid_low, -1, 0)
    yl = moved(jnp.concatenate([xl[-1:], grid[:, -1], xh[-1:]], axis=0), 0, 1)
    yh = moved(jnp.concatenate([xl[:1], grid[:, 0], xh[:1]], axis=0), 0, -1)
    act, coarse, act_low, act_high = call(
        first_conv_kernel,
        [
            ((TILE_X, TILE_Y, CHAN, LANES), BF),
            ((TILE_X // 2, TILE_Y // 2, CHAN, LANES), BF),
            ((2 * TILE_Y, CHAN, LANES), BF),
            ((2 * TILE_Y, CHAN, LANES), BF),
        ],
        [SM] + [VM] * 6,
        [pltpu.VMEM((TILE_X + 2, TILE_Y + 2, 3 * CHAN, LANES), BF)],
        1300000000,
    )(where, grid, xl, xh, yl, yh, in_weight)

    xl = moved(act_high, 1, 0)
    xh = moved(act_low, -1, 0)
    cxl = xl[TILE_Y:].reshape(2, 4, CHAN, LANES)
    cxh = xh[TILE_Y:].reshape(2, 4, CHAN, LANES)
    yl = moved(
        jnp.concatenate(
            [
                xl[TILE_Y - 1 : TILE_Y],
                act[:, -1],
                xh[TILE_Y - 1 : TILE_Y],
                jnp.concatenate([cxl[:, 2:], coarse[:, 2:], cxh[:, 2:]], axis=0).reshape(
                    12, CHAN, LANES
                ),
            ],
            axis=0,
        ),
        0,
        1,
    )
    yh = moved(
        jnp.concatenate(
            [
                xl[:1],
                act[:, 0],
                xh[:1],
                jnp.concatenate([cxl[:, :2], coarse[:, :2], cxh[:, :2]], axis=0).reshape(
                    12, CHAN, LANES
                ),
            ],
            axis=0,
        ),
        0,
        -1,
    )
    field = call(
        second_conv_kernel,
        [((3, TILE_X * TILE_Y, LANES), F32)],
        [SM] + [VM] * 8,
        [
            pltpu.VMEM((6, 8, 3 * CHAN, LANES), BF),
            pltpu.VMEM((TILE_X + 2, TILE_Y + 2, CHAN, LANES), BF),
            pltpu.VMEM((4, 6, CHAN, LANES), BF),
            pltpu.VMEM((TILE_X + 2, TILE_Y + 2, 27 * 8, LANES), F32),
        ],
        1300000000,
    )(where, act, coarse, xl, xh, yl, yh, mid_weight, out_weight)[0]

    xl = moved(field, 1, 0)
    xh = moved(field, -1, 0)
    row = jnp.stack([xl, field, xh], axis=0)
    yl = moved(row, 0, 1)
    yh = moved(row, 0, -1)
    return call(
        gather_kernel,
        [((blocks, 3, LANES), F32)],
        [SM] * 4 + [VM] * 7,
        [
            pltpu.VMEM((10, 3, TILE_X * TILE_Y, LANES), F32),
            pltpu.VMEM((blocks, 24, LANES), F32),
        ],
        70000000,
    )(
        where, block_counts, entry_block, dest, field, xl, xh, yl, yh, entry_nodes, entry_weights
    )[0]


def solution(mesh):
    in_specs = (
        P(("gx", "gy"), None, None),
        P(("gx", "gy")),
        P(("gx", "gy")),
        P(("gx", "gy"), None),
        P(("gx", "gy"), None),
        P(("gx", "gy"), None, None),
        P(),
        P(),
        P(),
        P(),
    )
    out_specs = P(("gx", "gy"), None, None)
    return jax.shard_map(shards, mesh=mesh, in_specs=in_specs, out_specs=out_specs, check_vma=False)
```

```python
import functools

import jax
import jax.numpy as jnp
from jax import lax
from jax.experimental import pallas as pl
from jax.experimental.pallas import tpu as pltpu
from jax.sharding import PartitionSpec as P

BF = jnp.bfloat16
F32 = jnp.float32
I32 = jnp.int32

CHAN = 64
LANES = 128
TILE_X = 4
TILE_Y = 8
SLOTS = 8
GROUP = 4
CHUNKS = 4
VMEM_LIMIT = 40 * 1024 * 1024

VM = pl.BlockSpec(memory_space=pltpu.VMEM)
SM = pl.BlockSpec(memory_space=pltpu.SMEM)
HB = pl.BlockSpec(memory_space=pltpu.HBM)
NT = (((1,), (1,)), ((), ()))


def call(kernel, outs, ins, scratch, flops, limit=VMEM_LIMIT):
    return pl.pallas_call(
        kernel,
        out_shape=[jax.ShapeDtypeStruct(s, d) for s, d in outs],
        in_specs=ins,
        out_specs=[VM] * len(outs),
        scratch_shapes=scratch,
        compiler_params=pltpu.CompilerParams(vmem_limit_bytes=limit),
        cost_estimate=pl.CostEstimate(flops=flops, bytes_accessed=2000000, transcendentals=0),
    )


def partial_kernel(
    where_ref, counts_ref, block_ref, dest_ref, feat_hbm, nodes_ref, weight_hbm, *rest
):
    outs = rest[:9]
    feat_ref, weight_ref, sem, part, hi_all, lo_all, index, taken, entry_of = rest[9:]
    entries = weight_ref.shape[0]
    size = entries // CHUNKS
    copies = [pltpu.make_async_copy(feat_hbm, feat_ref, sem.at[CHUNKS])]
    for c in range(CHUNKS):
        rows = pl.ds(c * size, size)
        copies.append(pltpu.make_async_copy(weight_hbm.at[rows], weight_ref.at[rows], sem.at[c]))
    for c in copies:
        c.start()
    nodes = nodes_ref[...]
    hi_all[...] = (nodes >> 8).astype(F32)
    lo_all[...] = (nodes & 255).astype(F32)
    index[...] = jnp.full(index.shape, -1.0, F32)
    for d in range(9):
        taken[d] = 0

    def place(e, carry):
        tile = dest_ref[e]
        step_x = tile // where_ref[2] - where_ref[0]
        step_y = tile % where_ref[2] - where_ref[1]
        odd_x = where_ref[0] % 2
        odd_y = where_ref[1] % 2
        by_x = jnp.where(step_x > 0, odd_x, 1 - odd_x)
        by_y = jnp.where(step_y > 0, odd_y, 1 - odd_y)
        d = jnp.where(step_x == step_y, 5 + by_x, 7 + by_x)
        d = jnp.where(step_y == 0, 1 + by_x, d)
        d = jnp.where(step_x == 0, jnp.where(step_y == 0, 0, 3 + by_y), d)
        s = taken[d]
        taken[d] = s + 1
        entry_of[d * SLOTS + s] = e
        index[pl.ds(d * 16 + s, 1), :] = hi_all[pl.ds(e, 1), :]
        index[pl.ds(d * 16 + 8 + s, 1), :] = lo_all[pl.ds(e, 1), :]
        return carry

    lax.fori_loop(0, entries, place, 0)
    copies[0].wait()
    lane = lax.broadcasted_iota(I32, (CHAN, LANES), 1)
    for e in range(entries):
        if e % size == 0:
            copies[1 + e // size].wait()
        block = block_ref[e]
        feat = jnp.where(lane < counts_ref[block], feat_ref[block].astype(F32), 0.0).astype(BF)
        value = jnp.dot(feat, weight_ref[e], preferred_element_type=F32)
        part[e] = value.astype(BF)
    for d in range(9):

        def copy(s, carry, d=d):
            outs[d][pl.ds(pl.multiple_of(s * CHAN, CHAN), CHAN), :] = part[entry_of[d * SLOTS + s]]
            return carry

        lax.fori_loop(0, taken[d], copy, 0)
        outs[d][SLOTS * CHAN :, :] = index[d * 16 : d * 16 + 16, :].astype(BF)


def scatter_kernel(parts, first, last, *refs):
    where_ref = refs[0]
    got = refs[1 : parts + 1]
    refs = refs[parts + 1 :]
    if not first:
        before = refs[0]
        refs = refs[1:]
    if last:
        grid_ref, one_ref, two_ref, values, index, hi_all, lo_all, acc = refs
    else:
        acc, values, index, hi_all, lo_all = refs
    hi_all[...] = jnp.full(hi_all.shape, -1.0, F32)
    lo_all[...] = jnp.full(lo_all.shape, -1.0, F32)
    counts = []
    for d in range(parts):
        rows = got[d][SLOTS * CHAN :, :].astype(F32)
        index[d * 16 : d * 16 + 16, :] = rows
        counts.append(jnp.sum(jnp.where(rows[0:8, 0:1] >= 0.0, 1.0, 0.0)).astype(I32))
    filled = jnp.int32(0)
    for d in range(parts):

        def copy(s, pos, d=d):
            values[pos] = got[d][pl.ds(pl.multiple_of(s * CHAN, CHAN), CHAN), :]
            hi_all[pl.ds(pos, 1), :] = index[pl.ds(d * 16 + s, 1), :]
            lo_all[pl.ds(pos, 1), :] = index[pl.ds(d * 16 + 8 + s, 1), :]
            return pos + 1

        filled = lax.fori_loop(0, counts[d], copy, filled)
    row = lax.broadcasted_iota(I32, (256, LANES), 0).astype(F32)
    if first:
        acc[...] = jnp.zeros(acc.shape, F32)
    else:
        acc[...] = before[...]

    def step(g, carry):
        left = [[] for _ in range(16)]
        right = []
        for j in range(GROUP):
            e = g * GROUP + j
            value = values[e]
            hi = jnp.broadcast_to(hi_all[pl.ds(e, 1), :], (CHAN, LANES)).astype(BF)
            lo = lo_all[pl.ds(e, 1), :]
            right.append(jnp.where(row == lo, 1.0, 0.0).astype(BF))
            for t in range(16):
                left[t].append(jnp.where(hi == jnp.array(t, BF), value, jnp.array(0, BF)))
        a = jnp.concatenate([jnp.concatenate(rows, axis=1) for rows in left], axis=0)
        b = jnp.concatenate(right, axis=1)
        acc[...] += lax.dot_general(a, b, NT, preferred_element_type=F32)
        return carry

    lax.fori_loop(0, (filled + GROUP - 1) // GROUP, step, 0)
    if not last:
        return
    for t in range(16):
        for half in range(2):
            column = acc[t * CHAN : (t + 1) * CHAN, half * LANES : (half + 1) * LANES].astype(BF)
            x = t // 4
            y = (t % 4) * 2 + half
            grid_ref[x, y] = column
    odd = where_ref[0] % 2

    @pl.when(odd == 0)
    def _():
        one_ref[...] = grid_ref[TILE_X - 1]
        two_ref[...] = grid_ref[0]

    @pl.when(odd == 1)
    def _():
        one_ref[...] = grid_ref[0]
        two_ref[...] = grid_ref[TILE_X - 1]


def scatter(where, parts, before, last):
    most = len(parts) * SLOTS + GROUP
    sums = ((16 * CHAN, 256), F32)
    first = before is None
    if last:
        outs = [((TILE_X, TILE_Y, CHAN, LANES), BF)] + [((TILE_Y, CHAN, LANES), BF)] * 2
    else:
        outs = [sums]
    return call(
        functools.partial(scatter_kernel, len(parts), first, last),
        outs,
        [SM] + [VM] * (len(parts) + (not first)),
        [
            pltpu.VMEM((most, CHAN, LANES), BF),
            pltpu.VMEM((len(parts) * 16, LANES), F32),
            pltpu.VMEM((most, LANES), F32),
            pltpu.VMEM((most, LANES), F32),
        ]
        + [pltpu.VMEM(*sums)] * last,
        800000000,
    )(where, *parts, *([] if first else [before]))


def shifted(column):
    lane = lax.broadcasted_iota(I32, column.shape, 1)
    wide = column.astype(F32)
    before = jnp.where(lane == 0, 0.0, pltpu.roll(wide, 1, 1)).astype(BF)
    after = jnp.where(lane == LANES - 1, 0.0, pltpu.roll(wide, LANES - 1, 1)).astype(BF)
    return jnp.concatenate([before, column, after], axis=0)


def conv_rows(picks, weight_ref, size_x, put):
    weight = weight_ref[...]
    sums = [None] * size_x
    for x in range(size_x + 2):
        rhs = jnp.concatenate(picks(x), axis=1)
        first = max(0, x - size_x + 1)
        last = min(2, x)
        prod = jnp.dot(weight[first * CHAN : (last + 1) * CHAN], rhs, preferred_element_type=F32)
        for a in range(first, last + 1):
            piece = prod[(a - first) * CHAN : (a - first + 1) * CHAN]
            out = x - a
            sums[out] = piece if sums[out] is None else sums[out] + piece
        if x >= 2:
            put(x - 2, sums[x - 2])
            sums[x - 2] = None


def flat(taps):
    return taps.reshape(9 * CHAN, LANES)


def silu(v):
    return v / (1.0 + jnp.exp(-v))


def edges(where_ref):
    x_lo = where_ref[0] > 0
    x_hi = where_ref[0] < where_ref[3] - 1
    y_lo = where_ref[1] > 0
    y_hi = where_ref[1] < where_ref[2] - 1
    return x_lo, x_hi, y_lo, y_hi


def in_order(odd, one_ref, two_ref, low_ref, high_ref):
    @pl.when(odd == 0)
    def _():
        one_ref[...] = high_ref[...]
        two_ref[...] = low_ref[...]

    @pl.when(odd == 1)
    def _():
        one_ref[...] = low_ref[...]
        two_ref[...] = high_ref[...]


def sorted_x(where_ref, one_ref, two_ref, xl_ref, xh_ref):
    x_lo, x_hi, _, _ = edges(where_ref)
    odd = where_ref[0] % 2 == 1
    for i in range(xl_ref.shape[0]):
        one = one_ref[i].astype(F32)
        two = two_ref[i].astype(F32)
        xl_ref[i] = jnp.where(x_lo, jnp.where(odd, one, two), 0.0).astype(BF)
        xh_ref[i] = jnp.where(x_hi, jnp.where(odd, two, one), 0.0).astype(BF)


def sorted_y(where_ref, one_ref, two_ref, i):
    _, _, y_lo, y_hi = edges(where_ref)
    odd = where_ref[1] % 2 == 1
    one = one_ref[i].astype(F32)
    two = two_ref[i].astype(F32)
    lower = jnp.where(y_lo, jnp.where(odd, one, two), 0.0).astype(BF)
    higher = jnp.where(y_hi, jnp.where(odd, two, one), 0.0).astype(BF)
    return lower, higher


def grid_side_kernel(
    where_ref, one_ref, two_ref, grid_ref, xl_ref, xh_ref, y_one_ref, y_two_ref, low, high
):
    sorted_x(where_ref, one_ref, two_ref, xl_ref, xh_ref)
    for ref, y in ((low, 0), (high, TILE_Y - 1)):
        ref[0] = xl_ref[y]
        for x in range(TILE_X):
            ref[x + 1] = grid_ref[x, y]
        ref[TILE_X + 1] = xh_ref[y]
    in_order(where_ref[1] % 2, y_one_ref, y_two_ref, low, high)


def coarse_side_kernel(
    where_ref, one_ref, two_ref, coarse_ref, down_ref, up_ref,
    xl_ref, xh_ref, y_one_ref, y_two_ref, low, high,
):
    sorted_x(where_ref, one_ref, two_ref, xl_ref, xh_ref)
    half_y = TILE_Y // 2
    for ref, y, own in ((low, 0, down_ref), (high, half_y - 2, up_ref)):
        for x in range(2):
            for k in range(2):
                ref[x * 2 + k] = xl_ref[x * half_y + y + k]
                ref[4 + x * 2 + k] = coarse_ref[x, y + k]
                ref[8 + x * 2 + k] = xh_ref[x * half_y + y + k]
        ref[12] = own[0]
        ref[13] = xl_ref[9]
        ref[14] = xh_ref[9]
    in_order(where_ref[1] % 2, y_one_ref, y_two_ref, low, high)


def field_side_kernel(where_ref, one_ref, two_ref, own_ref, row_ref):
    odd = where_ref[0] % 2
    row_ref[1] = own_ref[...]

    @pl.when(odd == 0)
    def _():
        row_ref[0] = two_ref[...]
        row_ref[2] = one_ref[...]

    @pl.when(odd == 1)
    def _():
        row_ref[0] = one_ref[...]
        row_ref[2] = two_ref[...]


def masked(column, *conditions):
    keep = functools.reduce(jnp.logical_and, conditions)
    return jnp.where(keep, column.astype(F32), 0.0).astype(BF)


def inner_conv_kernel(grid_ref, xl_ref, xh_ref, weight_ref, stack, act_ref):
    for y in range(TILE_Y):
        for x in range(TILE_X):
            stack[x + 1, y] = shifted(grid_ref[x, y])
        stack[0, y] = shifted(xl_ref[y])
        stack[TILE_X + 1, y] = shifted(xh_ref[y])
    for y in range(1, TILE_Y - 1, 2):

        def picks(x, y=y):
            return [flat(stack[x, y - 1 : y + 2]), flat(stack[x, y : y + 3])]

        def put(x, value, y=y):
            for k in range(2):
                part = value[:, k * LANES : (k + 1) * LANES]
                act_ref[x, y - 1 + k] = (silu(part) + grid_ref[x, y + k].astype(F32)).astype(BF)

        conv_rows(picks, weight_ref, TILE_X, put)


def joined(total):
    lane = lax.broadcasted_iota(I32, (8, LANES), 1)
    before = jnp.where(lane == 0, 0.0, pltpu.roll(total[0:8], 1, 1))
    after = jnp.where(lane == LANES - 1, 0.0, pltpu.roll(total[16:24], LANES - 1, 1))
    both = before + total[8:16] + after
    return both[0:3] + both[3:6]


def two_parts(value):
    high = value.astype(BF).astype(F32)
    return jnp.concatenate([high, value - high, jnp.zeros((2, LANES), F32)], axis=0)


def one_part(column, row):
    piece = column[row : row + 8]
    return piece[0:3] + piece[3:6]


def outer_conv_kernel(
    where_ref, grid_ref, stack, inner_ref, y_one_ref, y_two_ref, weight_ref, out_weight_ref,
    act_ref, coarse_ref, one_ref, two_ref, down_ref, up_ref, edge, taps, low_ref, high_ref,
):
    for x in range(TILE_X + 2):
        lower, higher = sorted_y(where_ref, y_one_ref, y_two_ref, x)
        edge[x, 0] = shifted(lower)
        edge[x, 1] = shifted(higher)
    last_y = TILE_Y - 1

    def picks(x):
        return [
            jnp.concatenate([edge[x, 0], stack[x, 0], stack[x, 1]], axis=0),
            jnp.concatenate([stack[x, last_y - 1], stack[x, last_y], edge[x, 1]], axis=0),
        ]

    def put(x, value):
        for k, y in enumerate((0, last_y)):
            part = value[:, k * LANES : (k + 1) * LANES]
            act_ref[x, y] = (silu(part) + grid_ref[x, y].astype(F32)).astype(BF)

    conv_rows(picks, weight_ref, TILE_X, put)
    for x in range(TILE_X):
        for y in range(1, last_y):
            act_ref[x, y] = inner_ref[x, y - 1]
    half_y = TILE_Y // 2
    for x in range(TILE_X // 2):
        for y in range(half_y):
            total = (
                act_ref[2 * x, 2 * y].astype(F32)
                + act_ref[2 * x, 2 * y + 1].astype(F32)
                + act_ref[2 * x + 1, 2 * y].astype(F32)
                + act_ref[2 * x + 1, 2 * y + 1].astype(F32)
            )
            result = (total * 0.25).astype(BF)
            coarse_ref[x, y] = result
            low_ref[x * half_y + y] = result
            high_ref[x * half_y + y] = result
    pairs = []
    for x in (0, TILE_X - 1):
        pairs += [((x, y), (x, y + 1)) for y in range(0, TILE_Y, 2)]
    pairs += [((1, y), (2, y)) for y in (0, last_y)]
    weight = out_weight_ref[...]
    for first, second in pairs:
        rhs = jnp.concatenate([act_ref[first], act_ref[second]], axis=1)
        prod = jnp.dot(weight, rhs, preferred_element_type=F32)
        taps[first] = prod[:, :LANES]
        taps[second] = prod[:, LANES:]

    def outside(cells):
        total = None
        for x, y, a, b in cells:
            if 0 <= x < TILE_X and 0 <= y < TILE_Y:
                start = (a * 3 + b) * 24
                piece = taps[x, y, start : start + 24, :]
                total = piece if total is None else total + piece
        return two_parts(joined(total))

    def column(pieces):
        rest = CHAN - 8 * len(pieces)
        if rest:
            pieces = pieces + [jnp.zeros((rest, LANES), F32)]
        return jnp.concatenate(pieces, axis=0).astype(BF)

    for ref, x, a in ((low_ref, 0, 2), (high_ref, TILE_X - 1, 0)):
        cells = [
            outside([(x, y + b - 1, a, b) for b in range(3)]) for y in range(-1, TILE_Y + 1)
        ]
        ref[8] = column(cells[1:-1])
        ref[9] = column([cells[0], cells[-1]])
    for ref, y, b in ((down_ref, 0, 2), (up_ref, last_y, 0)):
        ref[0] = column(
            [outside([(x + a - 1, y, a, b) for a in range(3)]) for x in range(TILE_X)]
        )
    in_order(where_ref[0] % 2, one_ref, two_ref, low_ref, high_ref)


def second_conv_kernel(
    where_ref, act_ref, coarse_ref, xl_ref, xh_ref, y_one_ref, y_two_ref,
    mid_weight_ref, out_weight_ref,
    field_ref, sent_ref, stack, merged, mid_ref, taps, yl_ref, yh_ref,
):
    for i in range(15):
        yl_ref[i], yh_ref[i] = sorted_y(where_ref, y_one_ref, y_two_ref, i)
    x_lo, x_hi, y_lo, y_hi = edges(where_ref)
    half_x = TILE_X // 2
    half_y = TILE_Y // 2
    for x in range(half_x):
        for y in range(half_y):
            stack[x + 2, y + 2] = shifted(coarse_ref[x, y])
            stack[x, y + 2] = shifted(xl_ref[x * half_y + y])
            stack[x + 2 + half_x, y + 2] = shifted(xh_ref[x * half_y + y])
    for x in range(half_x + 4):
        for y in range(2):
            stack[x, y] = shifted(yl_ref[x * 2 + y])
            stack[x, half_y + 2 + y] = shifted(yh_ref[x * 2 + y])
    for y in range(0, half_y + 2, 2):

        def picks(x, y=y):
            return [flat(stack[x, y : y + 3]), flat(stack[x, y + 1 : y + 4])]

        def put(x, value, y=y):
            result = silu(value).astype(BF)
            mid_ref[x, y] = result[:, :LANES]
            mid_ref[x, y + 1] = result[:, LANES:]

        conv_rows(picks, mid_weight_ref, half_x + 2, put)
    for x in range(TILE_X + 2):
        for y in range(TILE_Y + 2):
            more = ()
            if x == 0:
                more += (x_lo,)
            if x == TILE_X + 1:
                more += (x_hi,)
            if y == 0:
                more += (y_lo,)
            if y == TILE_Y + 1:
                more += (y_hi,)
            value = mid_ref[(x + 1) // 2, (y + 1) // 2]
            if more:
                merged[x, y] = masked(value, *more)
            else:
                merged[x, y] = (act_ref[x - 1, y - 1].astype(F32) + value.astype(F32)).astype(BF)
    weight = out_weight_ref[...]
    for x in range(TILE_X + 2):
        for y in range(0, TILE_Y + 2, 2):
            pair = jnp.concatenate([merged[x, y], merged[x, y + 1]], axis=1)
            prod = jnp.dot(weight, pair, preferred_element_type=F32)
            taps[x, y] = prod[:, :LANES]
            taps[x, y + 1] = prod[:, LANES:]

    def received(ref, place, row):
        return one_part(ref[place].astype(F32), row)

    for x in range(TILE_X):
        for y in range(TILE_Y):
            total = None
            for a in range(3):
                for b in range(3):
                    start = (a * 3 + b) * 24
                    piece = taps[x + a, y + b, start : start + 24, :]
                    total = piece if total is None else total + piece
            value = joined(total)
            x_ref = xl_ref if x == 0 else xh_ref
            y_ref = yl_ref if y == 0 else yh_ref
            on_x = x in (0, TILE_X - 1)
            on_y = y in (0, TILE_Y - 1)
            if on_x:
                value += received(x_ref, 8, y * 8)
            if on_y:
                value += received(y_ref, 12, x * 8)
            if on_x and on_y:
                value += received(y_ref, 13 + (x > 0), 8 if y == 0 else 0)
            for d in range(3):
                field_ref[d, x * TILE_Y + y : x * TILE_Y + y + 1, :] = value[d : d + 1]
    sent_ref[...] = field_ref[...].astype(BF)


def gather_kernel(
    where_ref, counts_ref, block_ref, dest_ref, own_ref, row_ref, y_one_ref, y_two_ref,
    nodes_ref, weight_ref, out_ref, frame, total,
):
    entries = weight_ref.shape[0]
    blocks = out_ref.shape[0]
    odd = where_ref[1] % 2 == 1
    frame[5] = own_ref[...]
    for i in range(3):
        one = y_one_ref[i].astype(F32)
        two = y_two_ref[i].astype(F32)
        frame[3 * i + 1] = jnp.where(odd, one, two)
        frame[3 * i + 3] = jnp.where(odd, two, one)
        if i != 1:
            frame[3 * i + 2] = row_ref[i].astype(F32)
    total[...] = jnp.zeros(total.shape, F32)
    sub = lax.broadcasted_iota(I32, (8, LANES), 0)
    for e in range(entries):
        tile = dest_ref[e]
        d = (tile // where_ref[2] - where_ref[0] + 1) * 3 + (tile % where_ref[2] - where_ref[1] + 1)
        node = jnp.broadcast_to(nodes_ref[e : e + 1, :], (8, LANES))
        z = node & (LANES - 1)
        column = node >> 7
        rows = []
        for c in range(3):
            picked = None
            for q in range(4):
                table = frame[d + 1, c, q * 8 : q * 8 + 8, :]
                value = jnp.take_along_axis(table, z, axis=1)
                value = jnp.where(column == sub + q * 8, value, 0.0)
                picked = value if picked is None else picked + value
            rows.append(picked)
        wide = jnp.concatenate(rows, axis=0)
        high = wide.astype(BF)
        low = (wide - high.astype(F32)).astype(BF)
        both = jnp.concatenate([high, low], axis=0)
        value = lax.dot_general(both, weight_ref[e], NT, preferred_element_type=F32)
        block = block_ref[e]
        total[block] += value[0:24] + value[24:48]
    lane = lax.broadcasted_iota(I32, (1, LANES), 1)
    for b in range(blocks):
        live = lane < counts_ref[b]
        for c in range(3):
            value = jnp.sum(total[b, c * 8 : c * 8 + 8, :], axis=0, keepdims=True)
            out_ref[b, c : c + 1, :] = jnp.where(live, value, 0.0)


def partners(size_x, size_y, step_x, step_y, parity):
    left = [(0, y) for y in range(size_y)]
    top = [(x, size_y - 1) for x in range(1, size_x)]
    right = [(size_x - 1, y) for y in reversed(range(size_y - 1))]
    bottom = [(x, 0) for x in reversed(range(1, size_x - 1))]
    rim = left + top + right + bottom
    if not step_x:
        rim = rim[size_y - 1 :] + rim[: size_y - 1]
    partner = {}
    for x in range(size_x):
        for y in range(size_y):
            sign = 1 if (x if step_x else y) % 2 == parity else -1
            to = (x + sign * step_x, y + sign * step_y)
            if 0 <= to[0] < size_x and 0 <= to[1] < size_y:
                partner[x, y] = to
    alone = [place for place in rim if place not in partner]
    for one, two in zip(alone[::2], alone[1::2]):
        partner[one] = two
        partner[two] = one
    return partner


def swapped(value, step_x, step_y, parity):
    size_x = lax.axis_size("gx")
    size_y = lax.axis_size("gy")
    partner = partners(size_x, size_y, step_x, step_y, parity)
    pairs = [
        (x * size_y + y, to_x * size_y + to_y) for (x, y), (to_x, to_y) in sorted(partner.items())
    ]
    return lax.ppermute(value, ("gx", "gy"), pairs)


def across_x(one, two):
    return swapped(one, 1, 0, 0), swapped(two, 1, 0, 1)


def across_y(one, two):
    return swapped(one, 0, 1, 0), swapped(two, 0, 1, 1)


def shards(
    particle_feat, block_counts, entry_block, entry_dest, entry_nodes, entry_weights,
    conv_in, conv_mid, conv_out, head_weight,
):
    size_x = lax.axis_size("gx")
    size_y = lax.axis_size("gy")
    where = jnp.stack(
        [
            lax.axis_index("gx").astype(I32),
            lax.axis_index("gy").astype(I32),
            jnp.int32(size_y),
            jnp.int32(size_x),
        ]
    )
    blocks = particle_feat.shape[0]
    entries = entry_weights.shape[0]
    dest = entry_dest.reshape(entries)
    in_weight = conv_in.reshape(3 * CHAN, 9 * CHAN)
    mid_weight = conv_mid.reshape(3 * CHAN, 9 * CHAN)
    folded = jnp.einsum(
        "do,aox->adx", head_weight, conv_out.astype(F32), precision=lax.Precision.HIGHEST
    )
    high = lax.reduce_precision(folded, 8, 7)
    both = jnp.concatenate([high, folded - high, jnp.zeros((3, 2, 9 * CHAN), F32)], axis=1)
    out_weight = (
        both.reshape(3, 8, 9, CHAN).transpose(0, 2, 1, 3).reshape(27 * 8, CHAN).astype(BF)
    )

    packed = (SLOTS * CHAN + 16, LANES)
    sent = call(
        partial_kernel,
        [(packed, BF)] * 9,
        [SM] * 4 + [HB, VM, HB],
        [
            pltpu.VMEM(particle_feat.shape, BF),
            pltpu.VMEM(entry_weights.shape, BF),
            pltpu.SemaphoreType.DMA((CHUNKS + 1,)),
            pltpu.VMEM((entries, CHAN, LANES), BF),
            pltpu.VMEM((entries, LANES), F32),
            pltpu.VMEM((entries, LANES), F32),
            pltpu.VMEM((9 * 16, LANES), F32),
            pltpu.SMEM((9,), I32),
            pltpu.SMEM((9 * SLOTS,), I32),
        ],
        70000000,
        limit=60 * 1024 * 1024,
    )(where, block_counts, entry_block, dest, particle_feat, entry_nodes, entry_weights)
    sides = [*across_x(sent[1], sent[2]), *across_y(sent[3], sent[4])]
    sums = scatter(where, [sent[0]], None, False)[0]
    *corners, sums = lax.optimization_barrier((*sent[5:], sums))
    corners = [
        swapped(value, 1, 1 - 2 * (i // 2), i % 2) for i, value in enumerate(corners)
    ]
    sums = scatter(where, sides, sums, False)[0]
    grid, one, two = scatter(where, corners, sums, True)

    column = (CHAN, LANES)
    one, two = across_x(one, two)
    xl, xh, one, two = call(
        grid_side_kernel,
        [((TILE_Y, *column), BF)] * 2 + [((TILE_X + 2, *column), BF)] * 2,
        [SM] + [VM] * 3,
        [pltpu.VMEM((TILE_X + 2, *column), BF)] * 2,
        1000000,
    )(where, one, two, grid)
    one, two = across_y(one, two)
    stack, inner = call(
        inner_conv_kernel,
        [
            ((TILE_X + 2, TILE_Y, 3 * CHAN, LANES), BF),
            ((TILE_X, TILE_Y - 2, CHAN, LANES), BF),
        ],
        [VM] * 4,
        [],
        1000000000,
    )(grid, xl, xh, in_weight)
    act, coarse, one, two, down, up = call(
        outer_conv_kernel,
        [
            ((TILE_X, TILE_Y, *column), BF),
            ((TILE_X // 2, TILE_Y // 2, *column), BF),
            ((10, *column), BF),
            ((10, *column), BF),
            ((1, *column), BF),
            ((1, *column), BF),
        ],
        [SM] + [VM] * 7,
        [
            pltpu.VMEM((TILE_X + 2, 2, 3 * CHAN, LANES), BF),
            pltpu.VMEM((TILE_X, TILE_Y, 27 * 8, LANES), F32),
            pltpu.VMEM((10, *column), BF),
            pltpu.VMEM((10, *column), BF),
        ],
        600000000,
    )(where, grid, stack, inner, one, two, in_weight, out_weight)

    one, two = across_x(one, two)
    xl, xh, one, two = call(
        coarse_side_kernel,
        [((10, *column), BF)] * 2 + [((15, *column), BF)] * 2,
        [SM] + [VM] * 5,
        [pltpu.VMEM((15, *column), BF)] * 2,
        1000000,
    )(where, one, two, coarse, down, up)
    one, two = across_y(one, two)
    field, rounded = call(
        second_conv_kernel,
        [((3, TILE_X * TILE_Y, LANES), F32), ((3, TILE_X * TILE_Y, LANES), BF)],
        [SM] + [VM] * 8,
        [
            pltpu.VMEM((6, 8, 3 * CHAN, LANES), BF),
            pltpu.VMEM((TILE_X + 2, TILE_Y + 2, CHAN, LANES), BF),
            pltpu.VMEM((4, 6, CHAN, LANES), BF),
            pltpu.VMEM((TILE_X + 2, TILE_Y + 2, 27 * 8, LANES), F32),
            pltpu.VMEM((15, *column), BF),
            pltpu.VMEM((15, *column), BF),
        ],
        1300000000,
    )(where, act, coarse, xl, xh, one, two, mid_weight, out_weight)

    one, two = across_x(rounded, rounded)
    row = call(
        field_side_kernel,
        [((3, 3, TILE_X * TILE_Y, LANES), BF)],
        [SM] + [VM] * 3,
        [],
        1000000,
    )(where, one, two, rounded)[0]
    one, two = across_y(row, row)
    return call(
        gather_kernel,
        [((blocks, 3, LANES), F32)],
        [SM] * 4 + [VM] * 6,
        [
            pltpu.VMEM((10, 3, TILE_X * TILE_Y, LANES), F32),
            pltpu.VMEM((blocks, 24, LANES), F32),
        ],
        70000000,
    )(
        where, block_counts, entry_block, dest, field, row, one, two, entry_nodes, entry_weights
    )[0]


def solution(mesh):
    in_specs = (
        P(("gx", "gy"), None, None),
        P(("gx", "gy")),
        P(("gx", "gy")),
        P(("gx", "gy"), None),
        P(("gx", "gy"), None),
        P(("gx", "gy"), None, None),
        P(),
        P(),
        P(),
        P(),
    )
    out_specs = P(("gx", "gy"), None, None)
    return jax.shard_map(shards, mesh=mesh, in_specs=in_specs, out_specs=out_specs, check_vma=False)
```

```python
import functools

import jax
import jax.numpy as jnp
from jax import lax
from jax.experimental import pallas as pl
from jax.experimental.pallas import tpu as pltpu
from jax.sharding import PartitionSpec as P

BF = jnp.bfloat16
F32 = jnp.float32
I32 = jnp.int32

CHAN = 64
LANES = 128
TILE_X = 4
TILE_Y = 8
SLOTS = 8
GROUP = 4
CHUNKS = 4
VMEM_LIMIT = 40 * 1024 * 1024

VM = pl.BlockSpec(memory_space=pltpu.VMEM)
SM = pl.BlockSpec(memory_space=pltpu.SMEM)
HB = pl.BlockSpec(memory_space=pltpu.HBM)
NT = (((1,), (1,)), ((), ()))


def call(kernel, outs, ins, scratch, flops, limit=VMEM_LIMIT):
    return pl.pallas_call(
        kernel,
        out_shape=[jax.ShapeDtypeStruct(s, d) for s, d in outs],
        in_specs=ins,
        out_specs=[VM] * len(outs),
        scratch_shapes=scratch,
        compiler_params=pltpu.CompilerParams(vmem_limit_bytes=limit),
        cost_estimate=pl.CostEstimate(flops=flops, bytes_accessed=2000000, transcendentals=0),
    )


def partial_kernel(
    counts_ref, block_ref, dest_ref, feat_hbm, nodes_ref, weight_hbm, *rest
):
    outs = rest[:9]
    feat_ref, weight_ref, sem, part, hi_all, lo_all, index, taken, entry_of = rest[9:]
    entries = weight_ref.shape[0]
    size = entries // CHUNKS
    copies = [pltpu.make_async_copy(feat_hbm, feat_ref, sem.at[CHUNKS])]
    for c in range(CHUNKS):
        rows = pl.ds(c * size, size)
        copies.append(pltpu.make_async_copy(weight_hbm.at[rows], weight_ref.at[rows], sem.at[c]))
    for c in copies:
        c.start()
    nodes = nodes_ref[...]
    hi_all[...] = (nodes >> 8).astype(F32)
    lo_all[...] = (nodes & 255).astype(F32)
    index[...] = jnp.full(index.shape, -1.0, F32)
    for d in range(9):
        taken[d] = 0

    def place(e, carry):
        tile = dest_ref[e]
        step_x = tile // lax.axis_size("gy") - lax.axis_index("gx")
        step_y = tile % lax.axis_size("gy") - lax.axis_index("gy")
        odd_x = lax.axis_index("gx") % 2
        odd_y = lax.axis_index("gy") % 2
        by_x = jnp.where(step_x > 0, odd_x, 1 - odd_x)
        by_y = jnp.where(step_y > 0, odd_y, 1 - odd_y)
        d = jnp.where(step_x == step_y, 5 + by_x, 7 + by_x)
        d = jnp.where(step_y == 0, 1 + by_x, d)
        d = jnp.where(step_x == 0, jnp.where(step_y == 0, 0, 3 + by_y), d)
        s = taken[d]
        taken[d] = s + 1
        entry_of[d * SLOTS + s] = e
        index[pl.ds(d * 16 + s, 1), :] = hi_all[pl.ds(e, 1), :]
        index[pl.ds(d * 16 + 8 + s, 1), :] = lo_all[pl.ds(e, 1), :]
        return carry

    lax.fori_loop(0, entries, place, 0)
    copies[0].wait()
    lane = lax.broadcasted_iota(I32, (CHAN, LANES), 1)
    for e in range(entries):
        if e % size == 0:
            copies[1 + e // size].wait()
        block = block_ref[e]
        feat = jnp.where(lane < counts_ref[block], feat_ref[block].astype(F32), 0.0).astype(BF)
        value = jnp.dot(feat, weight_ref[e], preferred_element_type=F32)
        part[e] = value.astype(BF)
    for d in range(9):

        def copy(s, carry, d=d):
            outs[d][pl.ds(pl.multiple_of(s * CHAN, CHAN), CHAN), :] = part[entry_of[d * SLOTS + s]]
            return carry

        lax.fori_loop(0, taken[d], copy, 0)
        outs[d][SLOTS * CHAN :, :] = index[d * 16 : d * 16 + 16, :].astype(BF)


def scatter_kernel(parts, first, last, *refs):
    got = refs[:parts]
    refs = refs[parts:]
    if not first:
        before = refs[0]
        refs = refs[1:]
    if last:
        grid_ref, one_ref, two_ref, values, index, hi_all, lo_all, acc = refs
    else:
        acc, values, index, hi_all, lo_all = refs
    hi_all[...] = jnp.full(hi_all.shape, -1.0, F32)
    lo_all[...] = jnp.full(lo_all.shape, -1.0, F32)
    counts = []
    for d in range(parts):
        rows = got[d][SLOTS * CHAN :, :].astype(F32)
        index[d * 16 : d * 16 + 16, :] = rows
        counts.append(jnp.sum(jnp.where(rows[0:8, 0:1] >= 0.0, 1.0, 0.0)).astype(I32))
    filled = jnp.int32(0)
    for d in range(parts):

        def copy(s, pos, d=d):
            values[pos] = got[d][pl.ds(pl.multiple_of(s * CHAN, CHAN), CHAN), :]
            hi_all[pl.ds(pos, 1), :] = index[pl.ds(d * 16 + s, 1), :]
            lo_all[pl.ds(pos, 1), :] = index[pl.ds(d * 16 + 8 + s, 1), :]
            return pos + 1

        filled = lax.fori_loop(0, counts[d], copy, filled)
    row = lax.broadcasted_iota(I32, (256, LANES), 0).astype(F32)
    if first:
        acc[...] = jnp.zeros(acc.shape, F32)
    else:
        acc[...] = before[...]

    def step(g, carry):
        left = [[] for _ in range(16)]
        right = []
        for j in range(GROUP):
            e = g * GROUP + j
            value = values[e]
            hi = jnp.broadcast_to(hi_all[pl.ds(e, 1), :], (CHAN, LANES)).astype(BF)
            lo = lo_all[pl.ds(e, 1), :]
            right.append(jnp.where(row == lo, 1.0, 0.0).astype(BF))
            for t in range(16):
                left[t].append(jnp.where(hi == jnp.array(t, BF), value, jnp.array(0, BF)))
        a = jnp.concatenate([jnp.concatenate(rows, axis=1) for rows in left], axis=0)
        b = jnp.concatenate(right, axis=1)
        acc[...] += lax.dot_general(a, b, NT, preferred_element_type=F32)
        return carry

    lax.fori_loop(0, (filled + GROUP - 1) // GROUP, step, 0)
    if not last:
        return
    for t in range(16):
        for half in range(2):
            column = acc[t * CHAN : (t + 1) * CHAN, half * LANES : (half + 1) * LANES].astype(BF)
            x = t // 4
            y = (t % 4) * 2 + half
            grid_ref[x, y] = column
    odd = lax.axis_index("gx") % 2

    @pl.when(odd == 0)
    def _():
        one_ref[...] = grid_ref[TILE_X - 1]
        two_ref[...] = grid_ref[0]

    @pl.when(odd == 1)
    def _():
        one_ref[...] = grid_ref[0]
        two_ref[...] = grid_ref[TILE_X - 1]


def scatter(parts, before, last):
    most = len(parts) * SLOTS + GROUP
    sums = ((16 * CHAN, 256), F32)
    first = before is None
    if last:
        outs = [((TILE_X, TILE_Y, CHAN, LANES), BF)] + [((TILE_Y, CHAN, LANES), BF)] * 2
    else:
        outs = [sums]
    return call(
        functools.partial(scatter_kernel, len(parts), first, last),
        outs,
        [VM] * (len(parts) + (not first)),
        [
            pltpu.VMEM((most, CHAN, LANES), BF),
            pltpu.VMEM((len(parts) * 16, LANES), F32),
            pltpu.VMEM((most, LANES), F32),
            pltpu.VMEM((most, LANES), F32),
        ]
        + [pltpu.VMEM(*sums)] * last,
        800000000,
    )(*parts, *([] if first else [before]))


def shifted(column):
    lane = lax.broadcasted_iota(I32, column.shape, 1)
    wide = column.astype(F32)
    before = jnp.where(lane == 0, 0.0, pltpu.roll(wide, 1, 1)).astype(BF)
    after = jnp.where(lane == LANES - 1, 0.0, pltpu.roll(wide, LANES - 1, 1)).astype(BF)
    return jnp.concatenate([before, column, after], axis=0)


def conv_rows(picks, weight_ref, size_x, put):
    weight = weight_ref[...]
    sums = [None] * size_x
    for x in range(size_x + 2):
        rhs = jnp.concatenate(picks(x), axis=1)
        first = max(0, x - size_x + 1)
        last = min(2, x)
        prod = jnp.dot(weight[first * CHAN : (last + 1) * CHAN], rhs, preferred_element_type=F32)
        for a in range(first, last + 1):
            piece = prod[(a - first) * CHAN : (a - first + 1) * CHAN]
            out = x - a
            sums[out] = piece if sums[out] is None else sums[out] + piece
        if x >= 2:
            put(x - 2, sums[x - 2])
            sums[x - 2] = None


def flat(taps):
    return taps.reshape(9 * CHAN, LANES)


def silu(v):
    return v / (1.0 + jnp.exp(-v))


def edges():
    index_x = lax.axis_index("gx")
    index_y = lax.axis_index("gy")
    x_lo = index_x > 0
    x_hi = index_x < lax.axis_size("gx") - 1
    y_lo = index_y > 0
    y_hi = index_y < lax.axis_size("gy") - 1
    return x_lo, x_hi, y_lo, y_hi


def in_order(odd, one_ref, two_ref, low_ref, high_ref):
    @pl.when(odd == 0)
    def _():
        one_ref[...] = high_ref[...]
        two_ref[...] = low_ref[...]

    @pl.when(odd == 1)
    def _():
        one_ref[...] = low_ref[...]
        two_ref[...] = high_ref[...]


def sorted_x(one_ref, two_ref, xl_ref, xh_ref):
    x_lo, x_hi, _, _ = edges()
    odd = lax.axis_index("gx") % 2 == 1
    for i in range(xl_ref.shape[0]):
        one = one_ref[i].astype(F32)
        two = two_ref[i].astype(F32)
        xl_ref[i] = jnp.where(x_lo, jnp.where(odd, one, two), 0.0).astype(BF)
        xh_ref[i] = jnp.where(x_hi, jnp.where(odd, two, one), 0.0).astype(BF)


def sorted_y(one_ref, two_ref, i):
    _, _, y_lo, y_hi = edges()
    odd = lax.axis_index("gy") % 2 == 1
    one = one_ref[i].astype(F32)
    two = two_ref[i].astype(F32)
    lower = jnp.where(y_lo, jnp.where(odd, one, two), 0.0).astype(BF)
    higher = jnp.where(y_hi, jnp.where(odd, two, one), 0.0).astype(BF)
    return lower, higher


def grid_side_kernel(
    one_ref, two_ref, grid_ref, xl_ref, xh_ref, y_one_ref, y_two_ref, low, high
):
    sorted_x(one_ref, two_ref, xl_ref, xh_ref)
    for ref, y in ((low, 0), (high, TILE_Y - 1)):
        ref[0] = xl_ref[y]
        for x in range(TILE_X):
            ref[x + 1] = grid_ref[x, y]
        ref[TILE_X + 1] = xh_ref[y]
    in_order(lax.axis_index("gy") % 2, y_one_ref, y_two_ref, low, high)


def coarse_side_kernel(
    one_ref, two_ref, coarse_ref, down_ref, up_ref,
    xl_ref, xh_ref, y_one_ref, y_two_ref, low, high,
):
    sorted_x(one_ref, two_ref, xl_ref, xh_ref)
    half_y = TILE_Y // 2
    left = xl_ref[8].astype(F32)
    right = xh_ref[8].astype(F32)
    for ref, y, own, row in ((low, 0, down_ref, 48), (high, half_y - 2, up_ref, 54)):
        for x in range(2):
            for k in range(2):
                ref[x * 2 + k] = xl_ref[x * half_y + y + k]
                ref[4 + x * 2 + k] = coarse_ref[x, y + k]
                ref[8 + x * 2 + k] = xh_ref[x * half_y + y + k]
        ref[12] = filled_up([own[...], left[row : row + 6], right[row : row + 6]])
    in_order(lax.axis_index("gy") % 2, y_one_ref, y_two_ref, low, high)


def field_side_kernel(one_ref, two_ref, own_ref, row_ref):
    odd = lax.axis_index("gx") % 2
    row_ref[1] = own_ref[...]

    @pl.when(odd == 0)
    def _():
        row_ref[0] = two_ref[...]
        row_ref[2] = one_ref[...]

    @pl.when(odd == 1)
    def _():
        row_ref[0] = one_ref[...]
        row_ref[2] = two_ref[...]


def masked(column, *conditions):
    keep = functools.reduce(jnp.logical_and, conditions)
    return jnp.where(keep, column.astype(F32), 0.0).astype(BF)


def inner_conv_kernel(grid_ref, xl_ref, xh_ref, weight_ref, stack, act_ref):
    for y in range(TILE_Y):
        for x in range(TILE_X):
            stack[x + 1, y] = shifted(grid_ref[x, y])
        stack[0, y] = shifted(xl_ref[y])
        stack[TILE_X + 1, y] = shifted(xh_ref[y])
    for y in range(1, TILE_Y - 1, 2):

        def picks(x, y=y):
            return [flat(stack[x, y - 1 : y + 2]), flat(stack[x, y : y + 3])]

        def put(x, value, y=y):
            for k in range(2):
                part = value[:, k * LANES : (k + 1) * LANES]
                act_ref[x, y - 1 + k] = (silu(part) + grid_ref[x, y + k].astype(F32)).astype(BF)

        conv_rows(picks, weight_ref, TILE_X, put)


def joined(total):
    lane = lax.broadcasted_iota(I32, (8, LANES), 1)
    before = jnp.where(lane == 0, 0.0, pltpu.roll(total[0:8], 1, 1))
    after = jnp.where(lane == LANES - 1, 0.0, pltpu.roll(total[16:24], LANES - 1, 1))
    both = before + total[8:16] + after
    return both[0:3] + both[3:6]


def two_parts(value):
    high = value.astype(BF).astype(F32)
    return jnp.concatenate([high, value - high], axis=0)


def filled_up(pieces):
    rest = CHAN - sum(piece.shape[0] for piece in pieces)
    return jnp.concatenate(pieces + [jnp.zeros((rest, LANES), F32)], axis=0).astype(BF)


def added(pieces):
    return functools.reduce(lambda one, two: one + two, pieces)


def outer_conv_kernel(
    grid_ref, stack, inner_ref, y_one_ref, y_two_ref, weight_ref, out_weight_ref,
    act_ref, coarse_ref, one_ref, two_ref, edge, taps, low_ref, high_ref,
):
    for x in range(TILE_X + 2):
        lower, higher = sorted_y(y_one_ref, y_two_ref, x)
        edge[x, 0] = shifted(lower)
        edge[x, 1] = shifted(higher)
    last_y = TILE_Y - 1

    def picks(x):
        return [
            jnp.concatenate([edge[x, 0], stack[x, 0], stack[x, 1]], axis=0),
            jnp.concatenate([stack[x, last_y - 1], stack[x, last_y], edge[x, 1]], axis=0),
        ]

    def put(x, value):
        for k, y in enumerate((0, last_y)):
            part = value[:, k * LANES : (k + 1) * LANES]
            act_ref[x, y] = (silu(part) + grid_ref[x, y].astype(F32)).astype(BF)

    conv_rows(picks, weight_ref, TILE_X, put)
    for x in range(TILE_X):
        for y in range(1, last_y):
            act_ref[x, y] = inner_ref[x, y - 1]
    half_y = TILE_Y // 2
    for x in range(TILE_X // 2):
        for y in range(half_y):
            total = (
                act_ref[2 * x, 2 * y].astype(F32)
                + act_ref[2 * x, 2 * y + 1].astype(F32)
                + act_ref[2 * x + 1, 2 * y].astype(F32)
                + act_ref[2 * x + 1, 2 * y + 1].astype(F32)
            )
            result = (total * 0.25).astype(BF)
            coarse_ref[x, y] = result
            low_ref[x * half_y + y] = result
            high_ref[x * half_y + y] = result
    for side, ref, x, a in ((0, low_ref, 0, 2), (1, high_ref, TILE_X - 1, 0)):
        weight = out_weight_ref[a * 72 : a * 72 + 72]
        for y in range(0, TILE_Y, 2):
            rhs = jnp.concatenate([act_ref[x, y], act_ref[x, y + 1]], axis=1)
            prod = jnp.dot(weight, rhs, preferred_element_type=F32)
            taps[side, y] = prod[:, :LANES]
            taps[side, y + 1] = prod[:, LANES:]
        cells = []
        for y in [*range(TILE_Y), -1, TILE_Y]:
            near = [(y + b - 1, b) for b in range(3) if 0 <= y + b - 1 < TILE_Y]
            total = added([taps[side, v, b * 24 : b * 24 + 24, :] for v, b in near])
            cells.append(two_parts(joined(total)))
        ref[8] = filled_up(cells)
    in_order(lax.axis_index("gx") % 2, one_ref, two_ref, low_ref, high_ref)


def rim_kernel(act_ref, out_weight_ref, down_ref, up_ref, taps):
    weight = out_weight_ref[...]
    for ref, y, b in ((down_ref, 0, 2), (up_ref, TILE_Y - 1, 0)):
        for x in range(0, TILE_X, 2):
            rhs = jnp.concatenate([act_ref[x, y], act_ref[x + 1, y]], axis=1)
            prod = jnp.dot(weight, rhs, preferred_element_type=F32)
            taps[x] = prod[:, :LANES]
            taps[x + 1] = prod[:, LANES:]
        cells = []
        for x in range(TILE_X):
            near = [(x + a - 1, (a * 3 + b) * 24) for a in range(3) if 0 <= x + a - 1 < TILE_X]
            total = added([taps[u, start : start + 24, :] for u, start in near])
            cells.append(two_parts(joined(total)))
        ref[...] = jnp.concatenate(cells, axis=0)


def put_taps(weight, taps, places, columns):
    for (one, two), pair in zip(zip(places[::2], places[1::2]), zip(columns[::2], columns[1::2])):
        prod = jnp.dot(weight, jnp.concatenate(pair, axis=1), preferred_element_type=F32)
        taps[one] = prod[:, :LANES]
        taps[two] = prod[:, LANES:]


def inner_mid_kernel(
    coarse_ref, xl_ref, xh_ref, act_ref, mid_weight_ref, out_weight_ref, stack, taps, mid_ref
):
    x_lo, x_hi, _, _ = edges()
    half_x = TILE_X // 2
    half_y = TILE_Y // 2
    for x in range(half_x):
        for y in range(half_y):
            stack[x + 2, y] = shifted(coarse_ref[x, y])
            stack[x, y] = shifted(xl_ref[x * half_y + y])
            stack[x + 2 + half_x, y] = shifted(xh_ref[x * half_y + y])

    def picks(x):
        return [flat(stack[x, 0:3]), flat(stack[x, 1:4])]

    def put(x, value):
        result = silu(value).astype(BF)
        mid_ref[x, 0] = result[:, :LANES]
        mid_ref[x, 1] = result[:, LANES:]

    conv_rows(picks, mid_weight_ref, half_x + 2, put)
    weight = out_weight_ref[...]
    for x in range(TILE_X + 2):
        columns = []
        for y in range(4):
            value = mid_ref[(x + 1) // 2, y // 2]
            if x == 0:
                columns.append(masked(value, x_lo))
            elif x == TILE_X + 1:
                columns.append(masked(value, x_hi))
            else:
                fine = act_ref[x - 1, y + 2].astype(F32)
                columns.append((fine + value.astype(F32)).astype(BF))
        put_taps(weight, taps, [(x, y) for y in range(4)], columns)


def outer_mid_kernel(
    act_ref, stack, inner, xl_ref, xh_ref, y_one_ref, y_two_ref, mid_weight_ref, out_weight_ref,
    field_ref, sent_ref, edge, mid_ref, taps, yl_ref, yh_ref,
):
    x_lo, x_hi, y_lo, y_hi = edges()
    half_x = TILE_X // 2
    for i in range(13):
        yl_ref[i], yh_ref[i] = sorted_y(y_one_ref, y_two_ref, i)
    for x in range(half_x + 4):
        for k in range(2):
            edge[x, k] = shifted(yl_ref[x * 2 + k])
            edge[x, 2 + k] = shifted(yh_ref[x * 2 + k])
    for side in range(2):

        def picks(x, side=side):
            if side == 0:
                near = [edge[x, 0], edge[x, 1], stack[x, 0], stack[x, 1]]
            else:
                near = [stack[x, 2], stack[x, 3], edge[x, 2], edge[x, 3]]
            return [jnp.concatenate(near[:3], axis=0), jnp.concatenate(near[1:], axis=0)]

        def put(x, value, side=side):
            result = silu(value).astype(BF)
            mid_ref[x, 2 * side] = result[:, :LANES]
            mid_ref[x, 2 * side + 1] = result[:, LANES:]

        conv_rows(picks, mid_weight_ref, half_x + 2, put)
    weight = out_weight_ref[...]
    rows = (-1, 0, 1, TILE_Y - 2, TILE_Y - 1, TILE_Y)
    for x in range(TILE_X + 2):
        columns = []
        for y, k in zip(rows, (0, 1, 1, 2, 2, 3)):
            value = mid_ref[(x + 1) // 2, k]
            more = ()
            if x == 0:
                more += (x_lo,)
            if x == TILE_X + 1:
                more += (x_hi,)
            if y < 0:
                more += (y_lo,)
            if y == TILE_Y:
                more += (y_hi,)
            if more:
                columns.append(masked(value, *more))
            else:
                fine = act_ref[x - 1, y].astype(F32)
                columns.append((fine + value.astype(F32)).astype(BF))
        put_taps(weight, taps, [(x, k) for k in range(6)], columns)

    def tap(x, y, start):
        if y in rows:
            return taps[x, rows.index(y), start : start + 24, :]
        return inner[x, y - 2, start : start + 24, :]

    def received(ref, place, row):
        piece = ref[place].astype(F32)[row : row + 6]
        return piece[0:3] + piece[3:6]

    for x in range(TILE_X):
        for y in range(TILE_Y):
            value = joined(
                added(
                    [
                        tap(x + a, y + b - 1, (a * 3 + b) * 24)
                        for a in range(3)
                        for b in range(3)
                    ]
                )
            )
            x_ref = xl_ref if x == 0 else xh_ref
            y_ref = yl_ref if y == 0 else yh_ref
            on_x = x in (0, TILE_X - 1)
            on_y = y in (0, TILE_Y - 1)
            if on_x:
                value += received(x_ref, 8, y * 6)
            if on_y:
                value += received(y_ref, 12, x * 6)
            if on_x and on_y:
                value += received(y_ref, 12, 24 if x == 0 else 30)
            for d in range(3):
                field_ref[d, x * TILE_Y + y : x * TILE_Y + y + 1, :] = value[d : d + 1]
    sent_ref[...] = field_ref[...].astype(BF)


def gather_kernel(
    counts_ref, block_ref, dest_ref, own_ref, row_ref, y_one_ref, y_two_ref,
    nodes_ref, weight_ref, out_ref, frame, total,
):
    entries = weight_ref.shape[0]
    blocks = out_ref.shape[0]
    odd = lax.axis_index("gy") % 2 == 1
    frame[5] = own_ref[...]
    for i in range(3):
        one = y_one_ref[i].astype(F32)
        two = y_two_ref[i].astype(F32)
        frame[3 * i + 1] = jnp.where(odd, one, two)
        frame[3 * i + 3] = jnp.where(odd, two, one)
        if i != 1:
            frame[3 * i + 2] = row_ref[i].astype(F32)
    total[...] = jnp.zeros(total.shape, F32)
    sub = lax.broadcasted_iota(I32, (8, LANES), 0)
    for e in range(entries):
        tile = dest_ref[e]
        d = (tile // lax.axis_size("gy") - lax.axis_index("gx") + 1) * 3 + (tile % lax.axis_size("gy") - lax.axis_index("gy") + 1)
        node = jnp.broadcast_to(nodes_ref[e : e + 1, :], (8, LANES))
        z = node & (LANES - 1)
        column = node >> 7
        rows = []
        for c in range(3):
            picked = None
            for q in range(4):
                table = frame[d + 1, c, q * 8 : q * 8 + 8, :]
                value = jnp.take_along_axis(table, z, axis=1)
                value = jnp.where(column == sub + q * 8, value, 0.0)
                picked = value if picked is None else picked + value
            rows.append(picked)
        wide = jnp.concatenate(rows, axis=0)
        high = wide.astype(BF)
        low = (wide - high.astype(F32)).astype(BF)
        both = jnp.concatenate([high, low], axis=0)
        value = lax.dot_general(both, weight_ref[e], NT, preferred_element_type=F32)
        block = block_ref[e]
        total[block] += value[0:24] + value[24:48]
    lane = lax.broadcasted_iota(I32, (1, LANES), 1)
    for b in range(blocks):
        live = lane < counts_ref[b]
        for c in range(3):
            value = jnp.sum(total[b, c * 8 : c * 8 + 8, :], axis=0, keepdims=True)
            out_ref[b, c : c + 1, :] = jnp.where(live, value, 0.0)


def partners(size_x, size_y, step_x, step_y, parity):
    left = [(0, y) for y in range(size_y)]
    top = [(x, size_y - 1) for x in range(1, size_x)]
    right = [(size_x - 1, y) for y in reversed(range(size_y - 1))]
    bottom = [(x, 0) for x in reversed(range(1, size_x - 1))]
    rim = left + top + right + bottom
    if not step_x:
        rim = rim[size_y - 1 :] + rim[: size_y - 1]
    partner = {}
    for x in range(size_x):
        for y in range(size_y):
            sign = 1 if (x if step_x else y) % 2 == parity else -1
            to = (x + sign * step_x, y + sign * step_y)
            if 0 <= to[0] < size_x and 0 <= to[1] < size_y:
                partner[x, y] = to
    alone = [place for place in rim if place not in partner]
    for one, two in zip(alone[::2], alone[1::2]):
        partner[one] = two
        partner[two] = one
    return partner


def swapped(value, step_x, step_y, parity):
    size_x = lax.axis_size("gx")
    size_y = lax.axis_size("gy")
    partner = partners(size_x, size_y, step_x, step_y, parity)
    pairs = [
        (x * size_y + y, to_x * size_y + to_y) for (x, y), (to_x, to_y) in sorted(partner.items())
    ]
    return lax.ppermute(value, ("gx", "gy"), pairs)


def across_x(one, two):
    return swapped(one, 1, 0, 0), swapped(two, 1, 0, 1)


def across_y(one, two):
    return swapped(one, 0, 1, 0), swapped(two, 0, 1, 1)


def shards(
    particle_feat, block_counts, entry_block, entry_dest, entry_nodes, entry_weights,
    conv_in, conv_mid, conv_out, head_weight,
):
    blocks = particle_feat.shape[0]
    entries = entry_weights.shape[0]
    dest = entry_dest.reshape(entries)
    in_weight = conv_in.reshape(3 * CHAN, 9 * CHAN)
    mid_weight = conv_mid.reshape(3 * CHAN, 9 * CHAN)
    folded = jnp.einsum(
        "do,aox->adx", head_weight, conv_out.astype(F32), precision=lax.Precision.HIGHEST
    )
    high = lax.reduce_precision(folded, 8, 7)
    both = jnp.concatenate([high, folded - high, jnp.zeros((3, 2, 9 * CHAN), F32)], axis=1)
    out_weight = (
        both.reshape(3, 8, 9, CHAN).transpose(0, 2, 1, 3).reshape(27 * 8, CHAN).astype(BF)
    )

    packed = (SLOTS * CHAN + 16, LANES)
    sent = call(
        partial_kernel,
        [(packed, BF)] * 9,
        [SM] * 3 + [HB, VM, HB],
        [
            pltpu.VMEM(particle_feat.shape, BF),
            pltpu.VMEM(entry_weights.shape, BF),
            pltpu.SemaphoreType.DMA((CHUNKS + 1,)),
            pltpu.VMEM((entries, CHAN, LANES), BF),
            pltpu.VMEM((entries, LANES), F32),
            pltpu.VMEM((entries, LANES), F32),
            pltpu.VMEM((9 * 16, LANES), F32),
            pltpu.SMEM((9,), I32),
            pltpu.SMEM((9 * SLOTS,), I32),
        ],
        70000000,
        limit=60 * 1024 * 1024,
    )(block_counts, entry_block, dest, particle_feat, entry_nodes, entry_weights)
    sides = [*across_x(sent[1], sent[2]), *across_y(sent[3], sent[4])]
    sums = scatter([sent[0]], None, False)[0]
    corners = sent[5:]
    corners = [
        swapped(value, 1, 1 - 2 * (i // 2), i % 2) for i, value in enumerate(corners)
    ]
    sums = scatter(sides, sums, False)[0]
    grid, one, two = scatter(corners, sums, True)

    column = (CHAN, LANES)
    one, two = across_x(one, two)
    xl, xh, one, two = call(
        grid_side_kernel,
        [((TILE_Y, *column), BF)] * 2 + [((TILE_X + 2, *column), BF)] * 2,
        [VM] * 3,
        [pltpu.VMEM((TILE_X + 2, *column), BF)] * 2,
        1000000,
    )(one, two, grid)
    one, two = across_y(one, two)
    stack, inner = call(
        inner_conv_kernel,
        [
            ((TILE_X + 2, TILE_Y, 3 * CHAN, LANES), BF),
            ((TILE_X, TILE_Y - 2, CHAN, LANES), BF),
        ],
        [VM] * 4,
        [],
        1000000000,
    )(grid, xl, xh, in_weight)
    act, coarse, one, two = call(
        outer_conv_kernel,
        [
            ((TILE_X, TILE_Y, *column), BF),
            ((TILE_X // 2, TILE_Y // 2, *column), BF),
            ((9, *column), BF),
            ((9, *column), BF),
        ],
        [VM] * 7,
        [
            pltpu.VMEM((TILE_X + 2, 2, 3 * CHAN, LANES), BF),
            pltpu.VMEM((2, TILE_Y, 72, LANES), F32),
            pltpu.VMEM((9, *column), BF),
            pltpu.VMEM((9, *column), BF),
        ],
        600000000,
    )(grid, stack, inner, one, two, in_weight, out_weight)

    one, two = across_x(one, two)
    down, up = call(
        rim_kernel,
        [((24, LANES), F32)] * 2,
        [VM] * 2,
        [pltpu.VMEM((TILE_X, 27 * 8, LANES), F32)],
        1000000000,
    )(act, out_weight)
    xl, xh, one, two = call(
        coarse_side_kernel,
        [((9, *column), BF)] * 2 + [((13, *column), BF)] * 2,
        [VM] * 5,
        [pltpu.VMEM((13, *column), BF)] * 2,
        1000000,
    )(one, two, coarse, down, up)
    one, two = across_y(one, two)
    stack, inner = call(
        inner_mid_kernel,
        [
            ((6, TILE_Y // 2, 3 * CHAN, LANES), BF),
            ((TILE_X + 2, 4, 27 * 8, LANES), F32),
        ],
        [VM] * 6,
        [pltpu.VMEM((4, 2, *column), BF)],
        1000000000,
    )(coarse, xl, xh, act, mid_weight, out_weight)
    field, rounded = call(
        outer_mid_kernel,
        [((3, TILE_X * TILE_Y, LANES), F32), ((3, TILE_X * TILE_Y, LANES), BF)],
        [VM] * 9,
        [
            pltpu.VMEM((6, 4, 3 * CHAN, LANES), BF),
            pltpu.VMEM((4, 4, *column), BF),
            pltpu.VMEM((TILE_X + 2, 6, 27 * 8, LANES), F32),
            pltpu.VMEM((13, *column), BF),
            pltpu.VMEM((13, *column), BF),
        ],
        1300000000,
    )(act, stack, inner, xl, xh, one, two, mid_weight, out_weight)

    one, two = across_x(rounded, rounded)
    row = call(
        field_side_kernel,
        [((3, 3, TILE_X * TILE_Y, LANES), BF)],
        [VM] * 3,
        [],
        1000000,
    )(one, two, rounded)[0]
    one, two = across_y(row, row)
    return call(
        gather_kernel,
        [((blocks, 3, LANES), F32)],
        [SM] * 3 + [VM] * 6,
        [
            pltpu.VMEM((10, 3, TILE_X * TILE_Y, LANES), F32),
            pltpu.VMEM((blocks, 24, LANES), F32),
        ],
        70000000,
    )(
        block_counts, entry_block, dest, field, row, one, two, entry_nodes, entry_weights
    )[0]


def solution(mesh):
    in_specs = (
        P(("gx", "gy"), None, None),
        P(("gx", "gy")),
        P(("gx", "gy")),
        P(("gx", "gy"), None),
        P(("gx", "gy"), None),
        P(("gx", "gy"), None, None),
        P(),
        P(),
        P(),
        P(),
    )
    out_specs = P(("gx", "gy"), None, None)
    return jax.shard_map(shards, mesh=mesh, in_specs=in_specs, out_specs=out_specs, check_vma=False)
```

```python
import functools

import jax
import jax.numpy as jnp
from jax import lax
from jax.experimental import pallas as pl
from jax.experimental.pallas import tpu as pltpu
from jax.sharding import PartitionSpec as P

BF = jnp.bfloat16
F32 = jnp.float32
I32 = jnp.int32

CHAN = 64
LANES = 128
TILE_X = 4
TILE_Y = 8
SLOTS = 8
GROUP = 4
CHUNKS = 4
OUTER = (0, TILE_X - 1)
MIDDLE = tuple(range(1, TILE_X - 1))
VMEM_LIMIT = 40 * 1024 * 1024

VM = pl.BlockSpec(memory_space=pltpu.VMEM)
SM = pl.BlockSpec(memory_space=pltpu.SMEM)
HB = pl.BlockSpec(memory_space=pltpu.HBM)
NT = (((1,), (1,)), ((), ()))


def call(kernel, outs, ins, scratch, flops, limit=VMEM_LIMIT, to=VM):
    return pl.pallas_call(
        kernel,
        out_shape=[jax.ShapeDtypeStruct(s, d) for s, d in outs],
        in_specs=ins,
        out_specs=[to] * len(outs),
        scratch_shapes=scratch,
        compiler_params=pltpu.CompilerParams(vmem_limit_bytes=limit),
        cost_estimate=pl.CostEstimate(flops=flops, bytes_accessed=2000000, transcendentals=0),
    )


def partial_kernel(
    counts_ref, block_ref, dest_ref, feat_hbm, nodes_ref, weight_hbm, *rest
):
    outs = rest[:9]
    feat_ref, weight_ref, sem, packed, hi_all, lo_all, index, taken = rest[9:]
    entries = weight_ref.shape[0]
    size = entries // CHUNKS
    copies = [pltpu.make_async_copy(feat_hbm, feat_ref, sem.at[CHUNKS])]
    for c in range(CHUNKS):
        rows = pl.ds(c * size, size)
        copies.append(pltpu.make_async_copy(weight_hbm.at[rows], weight_ref.at[rows], sem.at[c]))
    for c in copies:
        c.start()
    nodes = nodes_ref[...]
    hi_all[...] = (nodes >> 8).astype(F32)
    lo_all[...] = (nodes & 255).astype(F32)
    index[...] = jnp.full(index.shape, -1.0, F32)
    for d in range(9):
        taken[d] = 0
    index_x = lax.axis_index("gx")
    index_y = lax.axis_index("gy")
    odd_x = (index_x + 1) % 2
    odd_y = (index_y + 1) % 2
    lane = lax.broadcasted_iota(I32, (CHAN, LANES), 1)
    copies[0].wait()
    for e in range(entries):
        if e % size == 0:
            copies[1 + e // size].wait()
        tile = dest_ref[e]
        step_x = tile // lax.axis_size("gy") - index_x
        step_y = tile % lax.axis_size("gy") - index_y
        by_x = jnp.where(step_x > 0, odd_x, 1 - odd_x)
        by_y = jnp.where(step_y > 0, odd_y, 1 - odd_y)
        d = jnp.where(step_x == step_y, 5 + by_x, 7 + by_x)
        d = jnp.where(step_y == 0, 1 + by_x, d)
        d = jnp.where(step_x == 0, jnp.where(step_y == 0, 0, 3 + by_y), d)
        s = taken[d]
        taken[d] = s + 1
        index[pl.ds(d * 16 + s, 1), :] = hi_all[e : e + 1, :]
        index[pl.ds(d * 16 + 8 + s, 1), :] = lo_all[e : e + 1, :]
        block = block_ref[e]
        feat = jnp.where(lane < counts_ref[block], feat_ref[block].astype(F32), 0.0).astype(BF)
        value = jnp.dot(feat, weight_ref[e], preferred_element_type=F32)
        start = pl.multiple_of(s * CHAN, CHAN)
        packed[d, pl.ds(start, CHAN), :] = value.astype(BF)
    copies = []
    for d in (1, 2, 3, 4, 5, 6, 7, 8, 0):
        packed[d, SLOTS * CHAN :, :] = index[d * 16 : d * 16 + 16, :].astype(BF)
        copies.append(pltpu.make_async_copy(packed.at[d], outs[d], sem.at[CHUNKS + 1 + d]))
        copies[-1].start()
    for c in copies:
        c.wait()


def scatter_kernel(parts, first, rows, *refs):
    got = refs[:parts]
    refs = refs[parts:]
    if not first:
        before = refs[0]
        refs = refs[1:]
    if rows is None:
        acc, values, index, hi_all, lo_all = refs
        groups = list(range(16))
    else:
        grid_ref = refs[0]
        sides = refs[1:-5]
        values, index, hi_all, lo_all, acc = refs[-5:]
        groups = [4 * x + k for x in rows for k in range(4)]
    hi_all[...] = jnp.full(hi_all.shape, -1.0, F32)
    lo_all[...] = jnp.full(lo_all.shape, -1.0, F32)
    counts = []
    for d in range(parts):
        marks = got[d][SLOTS * CHAN :, :].astype(F32)
        index[d * 16 : d * 16 + 16, :] = marks
        counts.append(jnp.sum(jnp.where(marks[0:8, 0:1] >= 0.0, 1.0, 0.0)).astype(I32))
    filled = jnp.int32(0)
    for d in range(parts):

        def copy(s, pos, d=d):
            values[pos] = got[d][pl.ds(pl.multiple_of(s * CHAN, CHAN), CHAN), :]
            hi_all[pl.ds(pos, 1), :] = index[pl.ds(d * 16 + s, 1), :]
            lo_all[pl.ds(pos, 1), :] = index[pl.ds(d * 16 + 8 + s, 1), :]
            return pos + 1

        filled = lax.fori_loop(0, counts[d], copy, filled)
    row = lax.broadcasted_iota(I32, (256, LANES), 0).astype(F32)
    for i, t in enumerate(groups):
        piece = slice(i * CHAN, (i + 1) * CHAN)
        if first:
            acc[piece, :] = jnp.zeros((CHAN, 256), F32)
        else:
            acc[piece, :] = before[t * CHAN : (t + 1) * CHAN, :]

    def step(g, carry):
        left = [[] for _ in groups]
        right = []
        for j in range(GROUP):
            e = g * GROUP + j
            value = values[e]
            hi = jnp.broadcast_to(hi_all[pl.ds(e, 1), :], (CHAN, LANES)).astype(BF)
            lo = lo_all[pl.ds(e, 1), :]
            right.append(jnp.where(row == lo, 1.0, 0.0).astype(BF))
            for kept, t in zip(left, groups):
                kept.append(jnp.where(hi == jnp.array(t, BF), value, jnp.array(0, BF)))
        a = jnp.concatenate([jnp.concatenate(kept, axis=1) for kept in left], axis=0)
        b = jnp.concatenate(right, axis=1)
        acc[...] += lax.dot_general(a, b, NT, preferred_element_type=F32)
        return carry

    lax.fori_loop(0, (filled + GROUP - 1) // GROUP, step, 0)
    if rows is None:
        return
    for i in range(len(groups)):
        for half in range(2):
            column = acc[i * CHAN : (i + 1) * CHAN, half * LANES : (half + 1) * LANES].astype(BF)
            grid_ref[i // 4, (i % 4) * 2 + half] = column
    if sides:
        in_order((lax.axis_index("gx") + 1) % 2, *sides, grid_ref.at[0], grid_ref.at[1])


def scatter(parts, before, rows=None):
    most = len(parts) * SLOTS + GROUP
    sums = ((16 * CHAN, 256), F32)
    first = before is None
    if rows is None:
        outs = [sums]
        scratch = []
    else:
        outs = [((len(rows), TILE_Y, CHAN, LANES), BF)]
        if rows == OUTER:
            outs += [((TILE_Y, CHAN, LANES), BF)] * 2
        scratch = [pltpu.VMEM((len(rows) * 4 * CHAN, 256), F32)]
    return call(
        functools.partial(scatter_kernel, len(parts), first, rows),
        outs,
        [VM] * (len(parts) + (not first)),
        [
            pltpu.VMEM((most, CHAN, LANES), BF),
            pltpu.VMEM((len(parts) * 16, LANES), F32),
            pltpu.VMEM((most, LANES), F32),
            pltpu.VMEM((most, LANES), F32),
        ]
        + scratch,
        800000000,
    )(*parts, *([] if first else [before]))


def cell(outer_ref, middle_ref, x, y):
    return outer_ref[x // (TILE_X - 1), y] if x in OUTER else middle_ref[x - 1, y]


def shifted(column):
    lane = lax.broadcasted_iota(I32, column.shape, 1)
    wide = column.astype(F32)
    before = jnp.where(lane == 0, 0.0, pltpu.roll(wide, 1, 1)).astype(BF)
    after = jnp.where(lane == LANES - 1, 0.0, pltpu.roll(wide, LANES - 1, 1)).astype(BF)
    return jnp.concatenate([before, column, after], axis=0)


def conv_rows(picks, weight_ref, size_x, put):
    weight = weight_ref[...]
    sums = [None] * size_x
    for x in range(size_x + 2):
        rhs = jnp.concatenate(picks(x), axis=1)
        first = max(0, x - size_x + 1)
        last = min(2, x)
        prod = jnp.dot(weight[first * CHAN : (last + 1) * CHAN], rhs, preferred_element_type=F32)
        for a in range(first, last + 1):
            piece = prod[(a - first) * CHAN : (a - first + 1) * CHAN]
            out = x - a
            sums[out] = piece if sums[out] is None else sums[out] + piece
        if x >= 2:
            put(x - 2, sums[x - 2])
            sums[x - 2] = None


def flat(taps):
    return taps.reshape(9 * CHAN, LANES)


def silu(v):
    return v / (1.0 + jnp.exp(-v))


def edges():
    index_x = lax.axis_index("gx")
    index_y = lax.axis_index("gy")
    x_lo = index_x > 0
    x_hi = index_x < lax.axis_size("gx") - 1
    y_lo = index_y > 0
    y_hi = index_y < lax.axis_size("gy") - 1
    return x_lo, x_hi, y_lo, y_hi


def in_order(odd, one_ref, two_ref, low_ref, high_ref):
    @pl.when(odd == 0)
    def _():
        one_ref[...] = high_ref[...]
        two_ref[...] = low_ref[...]

    @pl.when(odd == 1)
    def _():
        one_ref[...] = low_ref[...]
        two_ref[...] = high_ref[...]


def sorted_x(one_ref, two_ref, xl_ref, xh_ref):
    x_lo, x_hi, _, _ = edges()
    odd = (lax.axis_index("gx") + 1) % 2 == 1
    for i in range(xl_ref.shape[0]):
        one = one_ref[i].astype(F32)
        two = two_ref[i].astype(F32)
        xl_ref[i] = jnp.where(x_lo, jnp.where(odd, one, two), 0.0).astype(BF)
        xh_ref[i] = jnp.where(x_hi, jnp.where(odd, two, one), 0.0).astype(BF)


def sorted_y(one_ref, two_ref, i):
    _, _, y_lo, y_hi = edges()
    odd = (lax.axis_index("gy") + 1) % 2 == 1
    one = one_ref[i].astype(F32)
    two = two_ref[i].astype(F32)
    lower = jnp.where(y_lo, jnp.where(odd, one, two), 0.0).astype(BF)
    higher = jnp.where(y_hi, jnp.where(odd, two, one), 0.0).astype(BF)
    return lower, higher


def grid_side_kernel(
    one_ref, two_ref, outer_ref, middle_ref, xl_ref, xh_ref, y_one_ref, y_two_ref, low, high
):
    sorted_x(one_ref, two_ref, xl_ref, xh_ref)
    for ref, y in ((low, 0), (high, TILE_Y - 1)):
        ref[0] = xl_ref[y]
        for x in range(TILE_X):
            ref[x + 1] = cell(outer_ref, middle_ref, x, y)
        ref[TILE_X + 1] = xh_ref[y]
    in_order((lax.axis_index("gy") + 1) % 2, y_one_ref, y_two_ref, low, high)


def coarse_side_kernel(
    one_ref, two_ref, coarse_ref, down_ref, up_ref,
    xl_ref, xh_ref, y_one_ref, y_two_ref, low, high,
):
    sorted_x(one_ref, two_ref, xl_ref, xh_ref)
    half_y = TILE_Y // 2
    left = xl_ref[8].astype(F32)
    right = xh_ref[8].astype(F32)
    for ref, y, own, row in ((low, 0, down_ref, 48), (high, half_y - 2, up_ref, 54)):
        for x in range(2):
            for k in range(2):
                ref[x * 2 + k] = xl_ref[x * half_y + y + k]
                ref[4 + x * 2 + k] = coarse_ref[x, y + k]
                ref[8 + x * 2 + k] = xh_ref[x * half_y + y + k]
        ref[12] = filled_up([own[...], left[row : row + 6], right[row : row + 6]])
    in_order((lax.axis_index("gy") + 1) % 2, y_one_ref, y_two_ref, low, high)


def field_side_kernel(one_ref, two_ref, own_ref, row_ref):
    odd = (lax.axis_index("gx") + 1) % 2
    row_ref[1] = own_ref[...]

    @pl.when(odd == 0)
    def _():
        row_ref[0] = two_ref[...]
        row_ref[2] = one_ref[...]

    @pl.when(odd == 1)
    def _():
        row_ref[0] = one_ref[...]
        row_ref[2] = two_ref[...]


def masked(column, *conditions):
    keep = functools.reduce(jnp.logical_and, conditions)
    return jnp.where(keep, column.astype(F32), 0.0).astype(BF)


def inner_conv_kernel(outer_ref, middle_ref, xl_ref, xh_ref, weight_ref, stack, act_ref):
    for y in range(TILE_Y):
        for x in range(TILE_X):
            stack[x + 1, y] = shifted(cell(outer_ref, middle_ref, x, y))
        stack[0, y] = shifted(xl_ref[y])
        stack[TILE_X + 1, y] = shifted(xh_ref[y])
    for y in range(1, TILE_Y - 1, 2):

        def picks(x, y=y):
            return [flat(stack[x, y - 1 : y + 2]), flat(stack[x, y : y + 3])]

        def put(x, value, y=y):
            for k in range(2):
                part = value[:, k * LANES : (k + 1) * LANES]
                own = cell(outer_ref, middle_ref, x, y + k).astype(F32)
                act_ref[x, y - 1 + k] = (silu(part) + own).astype(BF)

        conv_rows(picks, weight_ref, TILE_X, put)


def joined(total):
    lane = lax.broadcasted_iota(I32, (8, LANES), 1)
    before = jnp.where(lane == 0, 0.0, pltpu.roll(total[0:8], 1, 1))
    after = jnp.where(lane == LANES - 1, 0.0, pltpu.roll(total[16:24], LANES - 1, 1))
    both = before + total[8:16] + after
    return both[0:3] + both[3:6]


def two_parts(value):
    high = value.astype(BF).astype(F32)
    return jnp.concatenate([high, value - high], axis=0)


def filled_up(pieces):
    rest = CHAN - sum(piece.shape[0] for piece in pieces)
    return jnp.concatenate(pieces + [jnp.zeros((rest, LANES), F32)], axis=0).astype(BF)


def added(pieces):
    return functools.reduce(lambda one, two: one + two, pieces)


def outer_conv_kernel(
    outer_ref, middle_ref, stack, inner_ref, y_one_ref, y_two_ref, weight_ref, out_weight_ref,
    act_ref, coarse_ref, one_ref, two_ref, edge, taps, low_ref, high_ref,
):
    for x in range(TILE_X + 2):
        lower, higher = sorted_y(y_one_ref, y_two_ref, x)
        edge[x, 0] = shifted(lower)
        edge[x, 1] = shifted(higher)
    last_y = TILE_Y - 1

    def picks(x):
        return [
            jnp.concatenate([edge[x, 0], stack[x, 0], stack[x, 1]], axis=0),
            jnp.concatenate([stack[x, last_y - 1], stack[x, last_y], edge[x, 1]], axis=0),
        ]

    def put(x, value):
        for k, y in enumerate((0, last_y)):
            part = value[:, k * LANES : (k + 1) * LANES]
            own = cell(outer_ref, middle_ref, x, y).astype(F32)
            act_ref[x, y] = (silu(part) + own).astype(BF)

    conv_rows(picks, weight_ref, TILE_X, put)
    for x in range(TILE_X):
        for y in range(1, last_y):
            act_ref[x, y] = inner_ref[x, y - 1]
    half_y = TILE_Y // 2
    for x in range(TILE_X // 2):
        for y in range(half_y):
            total = (
                act_ref[2 * x, 2 * y].astype(F32)
                + act_ref[2 * x, 2 * y + 1].astype(F32)
                + act_ref[2 * x + 1, 2 * y].astype(F32)
                + act_ref[2 * x + 1, 2 * y + 1].astype(F32)
            )
            result = (total * 0.25).astype(BF)
            coarse_ref[x, y] = result
            low_ref[x * half_y + y] = result
            high_ref[x * half_y + y] = result
    for side, ref, x, a in ((0, low_ref, 0, 2), (1, high_ref, TILE_X - 1, 0)):
        weight = out_weight_ref[a * 72 : a * 72 + 72]
        for y in range(0, TILE_Y, 2):
            rhs = jnp.concatenate([act_ref[x, y], act_ref[x, y + 1]], axis=1)
            prod = jnp.dot(weight, rhs, preferred_element_type=F32)
            taps[side, y] = prod[:, :LANES]
            taps[side, y + 1] = prod[:, LANES:]
        cells = []
        for y in [*range(TILE_Y), -1, TILE_Y]:
            near = [(y + b - 1, b) for b in range(3) if 0 <= y + b - 1 < TILE_Y]
            total = added([taps[side, v, b * 24 : b * 24 + 24, :] for v, b in near])
            cells.append(two_parts(joined(total)))
        ref[8] = filled_up(cells)
    in_order((lax.axis_index("gx") + 1) % 2, one_ref, two_ref, low_ref, high_ref)


def rim_kernel(act_ref, out_weight_ref, down_ref, up_ref, taps):
    weight = out_weight_ref[...]
    for ref, y, b in ((down_ref, 0, 2), (up_ref, TILE_Y - 1, 0)):
        for x in range(0, TILE_X, 2):
            rhs = jnp.concatenate([act_ref[x, y], act_ref[x + 1, y]], axis=1)
            prod = jnp.dot(weight, rhs, preferred_element_type=F32)
            taps[x] = prod[:, :LANES]
            taps[x + 1] = prod[:, LANES:]
        cells = []
        for x in range(TILE_X):
            near = [(x + a - 1, (a * 3 + b) * 24) for a in range(3) if 0 <= x + a - 1 < TILE_X]
            total = added([taps[u, start : start + 24, :] for u, start in near])
            cells.append(two_parts(joined(total)))
        ref[...] = jnp.concatenate(cells, axis=0)


def put_taps(weight, taps, places, columns):
    for (one, two), pair in zip(zip(places[::2], places[1::2]), zip(columns[::2], columns[1::2])):
        prod = jnp.dot(weight, jnp.concatenate(pair, axis=1), preferred_element_type=F32)
        taps[one] = prod[:, :LANES]
        taps[two] = prod[:, LANES:]


def inner_mid_kernel(
    coarse_ref, xl_ref, xh_ref, act_ref, mid_weight_ref, out_weight_ref, stack, taps, mid_ref
):
    x_lo, x_hi, _, _ = edges()
    half_x = TILE_X // 2
    half_y = TILE_Y // 2
    for x in range(half_x):
        for y in range(half_y):
            stack[x + 2, y] = shifted(coarse_ref[x, y])
            stack[x, y] = shifted(xl_ref[x * half_y + y])
            stack[x + 2 + half_x, y] = shifted(xh_ref[x * half_y + y])

    def picks(x):
        return [flat(stack[x, 0:3]), flat(stack[x, 1:4])]

    def put(x, value):
        result = silu(value).astype(BF)
        mid_ref[x, 0] = result[:, :LANES]
        mid_ref[x, 1] = result[:, LANES:]

    conv_rows(picks, mid_weight_ref, half_x + 2, put)
    weight = out_weight_ref[...]
    for x in range(TILE_X + 2):
        columns = []
        for y in range(4):
            value = mid_ref[(x + 1) // 2, y // 2]
            if x == 0:
                columns.append(masked(value, x_lo))
            elif x == TILE_X + 1:
                columns.append(masked(value, x_hi))
            else:
                fine = act_ref[x - 1, y + 2].astype(F32)
                columns.append((fine + value.astype(F32)).astype(BF))
        put_taps(weight, taps, [(x, y) for y in range(4)], columns)


def outer_mid_kernel(
    act_ref, stack, inner, xl_ref, xh_ref, y_one_ref, y_two_ref, mid_weight_ref, out_weight_ref,
    field_ref, sent_ref, edge, mid_ref, taps, yl_ref, yh_ref,
):
    x_lo, x_hi, y_lo, y_hi = edges()
    half_x = TILE_X // 2
    for i in range(13):
        yl_ref[i], yh_ref[i] = sorted_y(y_one_ref, y_two_ref, i)
    for x in range(half_x + 4):
        for k in range(2):
            edge[x, k] = shifted(yl_ref[x * 2 + k])
            edge[x, 2 + k] = shifted(yh_ref[x * 2 + k])
    for side in range(2):

        def picks(x, side=side):
            if side == 0:
                near = [edge[x, 0], edge[x, 1], stack[x, 0], stack[x, 1]]
            else:
                near = [stack[x, 2], stack[x, 3], edge[x, 2], edge[x, 3]]
            return [jnp.concatenate(near[:3], axis=0), jnp.concatenate(near[1:], axis=0)]

        def put(x, value, side=side):
            result = silu(value).astype(BF)
            mid_ref[x, 2 * side] = result[:, :LANES]
            mid_ref[x, 2 * side + 1] = result[:, LANES:]

        conv_rows(picks, mid_weight_ref, half_x + 2, put)
    weight = out_weight_ref[...]
    rows = (-1, 0, 1, TILE_Y - 2, TILE_Y - 1, TILE_Y)
    for x in range(TILE_X + 2):
        columns = []
        for y, k in zip(rows, (0, 1, 1, 2, 2, 3)):
            value = mid_ref[(x + 1) // 2, k]
            more = ()
            if x == 0:
                more += (x_lo,)
            if x == TILE_X + 1:
                more += (x_hi,)
            if y < 0:
                more += (y_lo,)
            if y == TILE_Y:
                more += (y_hi,)
            if more:
                columns.append(masked(value, *more))
            else:
                fine = act_ref[x - 1, y].astype(F32)
                columns.append((fine + value.astype(F32)).astype(BF))
        put_taps(weight, taps, [(x, k) for k in range(6)], columns)

    def tap(x, y, start):
        if y in rows:
            return taps[x, rows.index(y), start : start + 24, :]
        return inner[x, y - 2, start : start + 24, :]

    def received(ref, place, row):
        piece = ref[place].astype(F32)[row : row + 6]
        return piece[0:3] + piece[3:6]

    for x in range(TILE_X):
        for y in range(TILE_Y):
            value = joined(
                added(
                    [
                        tap(x + a, y + b - 1, (a * 3 + b) * 24)
                        for a in range(3)
                        for b in range(3)
                    ]
                )
            )
            x_ref = xl_ref if x == 0 else xh_ref
            y_ref = yl_ref if y == 0 else yh_ref
            on_x = x in (0, TILE_X - 1)
            on_y = y in (0, TILE_Y - 1)
            if on_x:
                value += received(x_ref, 8, y * 6)
            if on_y:
                value += received(y_ref, 12, x * 6)
            if on_x and on_y:
                value += received(y_ref, 12, 24 if x == 0 else 30)
            for d in range(3):
                field_ref[d, x * TILE_Y + y : x * TILE_Y + y + 1, :] = value[d : d + 1]
    sent_ref[...] = field_ref[...].astype(BF)


def gather_kernel(
    counts_ref, block_ref, dest_ref, own_ref, row_ref, y_one_ref, y_two_ref,
    nodes_ref, weight_ref, out_ref, frame, total,
):
    entries = weight_ref.shape[0]
    blocks = out_ref.shape[0]
    odd = (lax.axis_index("gy") + 1) % 2 == 1
    frame[5] = own_ref[...]
    for i in range(3):
        one = y_one_ref[i].astype(F32)
        two = y_two_ref[i].astype(F32)
        frame[3 * i + 1] = jnp.where(odd, one, two)
        frame[3 * i + 3] = jnp.where(odd, two, one)
        if i != 1:
            frame[3 * i + 2] = row_ref[i].astype(F32)
    total[...] = jnp.zeros(total.shape, F32)
    sub = lax.broadcasted_iota(I32, (8, LANES), 0)
    for e in range(entries):
        tile = dest_ref[e]
        d = (tile // lax.axis_size("gy") - lax.axis_index("gx") + 1) * 3 + (tile % lax.axis_size("gy") - lax.axis_index("gy") + 1)
        node = jnp.broadcast_to(nodes_ref[e : e + 1, :], (8, LANES))
        z = node & (LANES - 1)
        column = node >> 7
        rows = []
        for c in range(3):
            picked = None
            for q in range(4):
                table = frame[d + 1, c, q * 8 : q * 8 + 8, :]
                value = jnp.take_along_axis(table, z, axis=1)
                value = jnp.where(column == sub + q * 8, value, 0.0)
                picked = value if picked is None else picked + value
            rows.append(picked)
        wide = jnp.concatenate(rows, axis=0)
        high = wide.astype(BF)
        low = (wide - high.astype(F32)).astype(BF)
        both = jnp.concatenate([high, low], axis=0)
        value = lax.dot_general(both, weight_ref[e], NT, preferred_element_type=F32)
        block = block_ref[e]
        total[block] += value[0:24] + value[24:48]
    lane = lax.broadcasted_iota(I32, (1, LANES), 1)
    for b in range(blocks):
        live = lane < counts_ref[b]
        for c in range(3):
            value = jnp.sum(total[b, c * 8 : c * 8 + 8, :], axis=0, keepdims=True)
            out_ref[b, c : c + 1, :] = jnp.where(live, value, 0.0)


def partners(size_x, size_y, step_x, step_y, parity):
    left = [(0, y) for y in range(size_y)]
    top = [(x, size_y - 1) for x in range(1, size_x)]
    right = [(size_x - 1, y) for y in reversed(range(size_y - 1))]
    bottom = [(x, 0) for x in reversed(range(1, size_x - 1))]
    rim = left + top + right + bottom
    if not step_x:
        rim = rim[size_y - 1 :] + rim[: size_y - 1]
    partner = {}
    for x in range(size_x):
        for y in range(size_y):
            sign = 1 if (x if step_x else y) % 2 == parity else -1
            to = (x + sign * step_x, y + sign * step_y)
            if 0 <= to[0] < size_x and 0 <= to[1] < size_y:
                partner[x, y] = to
    alone = [place for place in rim if place not in partner]
    for one, two in zip(alone[::2], alone[1::2]):
        partner[one] = two
        partner[two] = one
    return partner


def swapped(value, step_x, step_y, parity):
    size_x = lax.axis_size("gx")
    size_y = lax.axis_size("gy")
    partner = partners(size_x, size_y, step_x, step_y, parity)
    pairs = [
        (x * size_y + y, to_x * size_y + to_y) for (x, y), (to_x, to_y) in sorted(partner.items())
    ]
    return lax.ppermute(value, ("gx", "gy"), pairs)


def across_x(one, two):
    return swapped(one, 1, 0, 1), swapped(two, 1, 0, 0)


def across_y(one, two):
    return swapped(one, 0, 1, 1), swapped(two, 0, 1, 0)


def shards(
    particle_feat, block_counts, entry_block, entry_dest, entry_nodes, entry_weights,
    conv_in, conv_mid, conv_out, head_weight,
):
    blocks = particle_feat.shape[0]
    entries = entry_weights.shape[0]
    dest = entry_dest.reshape(entries)
    in_weight = conv_in.reshape(3 * CHAN, 9 * CHAN)
    mid_weight = conv_mid.reshape(3 * CHAN, 9 * CHAN)
    folded = jnp.einsum(
        "do,aox->adx", head_weight, conv_out.astype(F32), precision=lax.Precision.HIGHEST
    )
    high = lax.reduce_precision(folded, 8, 7)
    both = jnp.concatenate([high, folded - high, jnp.zeros((3, 2, 9 * CHAN), F32)], axis=1)
    out_weight = (
        both.reshape(3, 8, 9, CHAN).transpose(0, 2, 1, 3).reshape(27 * 8, CHAN).astype(BF)
    )

    packed = (SLOTS * CHAN + 16, LANES)
    sent = call(
        partial_kernel,
        [(packed, BF)] * 9,
        [SM] * 3 + [HB, VM, HB],
        [
            pltpu.VMEM(particle_feat.shape, BF),
            pltpu.VMEM(entry_weights.shape, BF),
            pltpu.SemaphoreType.DMA((CHUNKS + 10,)),
            pltpu.VMEM((9, *packed), BF),
            pltpu.VMEM((entries, LANES), F32),
            pltpu.VMEM((entries, LANES), F32),
            pltpu.VMEM((9 * 16, LANES), F32),
            pltpu.SMEM((9,), I32),
        ],
        70000000,
        limit=60 * 1024 * 1024,
        to=HB,
    )(block_counts, entry_block, dest, particle_feat, entry_nodes, entry_weights)
    sides = [*across_x(sent[1], sent[2]), *across_y(sent[3], sent[4])]
    sums = scatter([sent[0]], None)[0]
    corners = sent[5:]
    corners = [
        swapped(value, 1, 1 - 2 * (i // 2), 1 - i % 2) for i, value in enumerate(corners)
    ]
    sums = scatter([*sides, *corners[:2]], sums)[0]
    outer, one, two = scatter(corners[2:], sums, OUTER)
    middle = scatter(corners[2:], sums, MIDDLE)[0]

    column = (CHAN, LANES)
    one, two = across_x(one, two)
    xl, xh, one, two = call(
        grid_side_kernel,
        [((TILE_Y, *column), BF)] * 2 + [((TILE_X + 2, *column), BF)] * 2,
        [VM] * 4,
        [pltpu.VMEM((TILE_X + 2, *column), BF)] * 2,
        1000000,
    )(one, two, outer, middle)
    one, two = across_y(one, two)
    stack, inner = call(
        inner_conv_kernel,
        [
            ((TILE_X + 2, TILE_Y, 3 * CHAN, LANES), BF),
            ((TILE_X, TILE_Y - 2, CHAN, LANES), BF),
        ],
        [VM] * 5,
        [],
        1000000000,
    )(outer, middle, xl, xh, in_weight)
    act, coarse, one, two = call(
        outer_conv_kernel,
        [
            ((TILE_X, TILE_Y, *column), BF),
            ((TILE_X // 2, TILE_Y // 2, *column), BF),
            ((9, *column), BF),
            ((9, *column), BF),
        ],
        [VM] * 8,
        [
            pltpu.VMEM((TILE_X + 2, 2, 3 * CHAN, LANES), BF),
            pltpu.VMEM((2, TILE_Y, 72, LANES), F32),
            pltpu.VMEM((9, *column), BF),
            pltpu.VMEM((9, *column), BF),
        ],
        600000000,
    )(outer, middle, stack, inner, one, two, in_weight, out_weight)

    one, two = across_x(one, two)
    down, up = call(
        rim_kernel,
        [((24, LANES), F32)] * 2,
        [VM] * 2,
        [pltpu.VMEM((TILE_X, 27 * 8, LANES), F32)],
        1000000000,
    )(act, out_weight)
    xl, xh, one, two = call(
        coarse_side_kernel,
        [((9, *column), BF)] * 2 + [((13, *column), BF)] * 2,
        [VM] * 5,
        [pltpu.VMEM((13, *column), BF)] * 2,
        1000000,
    )(one, two, coarse, down, up)
    one, two = across_y(one, two)
    stack, inner = call(
        inner_mid_kernel,
        [
            ((6, TILE_Y // 2, 3 * CHAN, LANES), BF),
            ((TILE_X + 2, 4, 27 * 8, LANES), F32),
        ],
        [VM] * 6,
        [pltpu.VMEM((4, 2, *column), BF)],
        1000000000,
    )(coarse, xl, xh, act, mid_weight, out_weight)
    field, rounded = call(
        outer_mid_kernel,
        [((3, TILE_X * TILE_Y, LANES), F32), ((3, TILE_X * TILE_Y, LANES), BF)],
        [VM] * 9,
        [
            pltpu.VMEM((6, 4, 3 * CHAN, LANES), BF),
            pltpu.VMEM((4, 4, *column), BF),
            pltpu.VMEM((TILE_X + 2, 6, 27 * 8, LANES), F32),
            pltpu.VMEM((13, *column), BF),
            pltpu.VMEM((13, *column), BF),
        ],
        1300000000,
    )(act, stack, inner, xl, xh, one, two, mid_weight, out_weight)

    one, two = across_x(rounded, rounded)
    row = call(
        field_side_kernel,
        [((3, 3, TILE_X * TILE_Y, LANES), BF)],
        [VM] * 3,
        [],
        1000000,
    )(one, two, rounded)[0]
    one, two = across_y(row, row)
    return call(
        gather_kernel,
        [((blocks, 3, LANES), F32)],
        [SM] * 3 + [VM] * 6,
        [
            pltpu.VMEM((10, 3, TILE_X * TILE_Y, LANES), F32),
            pltpu.VMEM((blocks, 24, LANES), F32),
        ],
        70000000,
    )(
        block_counts, entry_block, dest, field, row, one, two, entry_nodes, entry_weights
    )[0]


def solution(mesh):
    in_specs = (
        P(("gx", "gy"), None, None),
        P(("gx", "gy")),
        P(("gx", "gy")),
        P(("gx", "gy"), None),
        P(("gx", "gy"), None),
        P(("gx", "gy"), None, None),
        P(),
        P(),
        P(),
        P(),
    )
    out_specs = P(("gx", "gy"), None, None)
    return jax.shard_map(shards, mesh=mesh, in_specs=in_specs, out_specs=out_specs, check_vma=False)
```

```python
import functools

import jax
import jax.numpy as jnp
from jax import lax
from jax.experimental import pallas as pl
from jax.experimental.pallas import tpu as pltpu
from jax.sharding import PartitionSpec as P

BF = jnp.bfloat16
F32 = jnp.float32
I32 = jnp.int32

CHAN = 64
LANES = 128
TILE_X = 4
TILE_Y = 8
SLOTS = 8
CHUNKS = 4
PADDED = 224
OUTER = (0, TILE_X - 1)
MIDDLE = tuple(range(1, TILE_X - 1))
VMEM_LIMIT = 40 * 1024 * 1024

VM = pl.BlockSpec(memory_space=pltpu.VMEM)
SM = pl.BlockSpec(memory_space=pltpu.SMEM)
HB = pl.BlockSpec(memory_space=pltpu.HBM)
NT = (((1,), (1,)), ((), ()))


def call(kernel, outs, ins, scratch, flops, limit=VMEM_LIMIT, to=VM):
    return pl.pallas_call(
        kernel,
        out_shape=[jax.ShapeDtypeStruct(s, d) for s, d in outs],
        in_specs=ins,
        out_specs=[to] * len(outs),
        scratch_shapes=scratch,
        compiler_params=pltpu.CompilerParams(vmem_limit_bytes=limit),
        cost_estimate=pl.CostEstimate(flops=flops, bytes_accessed=2000000, transcendentals=0),
    )


def partial_kernel(
    counts_ref, block_ref, dest_ref, feat_hbm, nodes_ref, weight_hbm, *rest
):
    outs = rest[:9]
    feat_ref, weight_ref, sem, packed, hi_all, lo_all, index, taken = rest[9:]
    entries = weight_ref.shape[0]
    size = entries // CHUNKS
    copies = [pltpu.make_async_copy(feat_hbm, feat_ref, sem.at[CHUNKS])]
    for c in range(CHUNKS):
        rows = pl.ds(c * size, size)
        copies.append(pltpu.make_async_copy(weight_hbm.at[rows], weight_ref.at[rows], sem.at[c]))
    for c in copies:
        c.start()
    nodes = nodes_ref[...]
    hi_all[...] = (nodes >> 8).astype(F32)
    lo_all[...] = (nodes & 255).astype(F32)
    index[...] = jnp.full(index.shape, -1.0, F32)
    for d in range(9):
        taken[d] = 0
    index_x = lax.axis_index("gx")
    index_y = lax.axis_index("gy")
    odd_x = (index_x + 1) % 2
    odd_y = (index_y + 1) % 2
    lane = lax.broadcasted_iota(I32, (CHAN, LANES), 1)
    copies[0].wait()
    for e in range(entries):
        if e % size == 0:
            copies[1 + e // size].wait()
        tile = dest_ref[e]
        step_x = tile // lax.axis_size("gy") - index_x
        step_y = tile % lax.axis_size("gy") - index_y
        by_x = jnp.where(step_x > 0, odd_x, 1 - odd_x)
        by_y = jnp.where(step_y > 0, odd_y, 1 - odd_y)
        d = jnp.where(step_x == step_y, 5 + by_x, 7 + by_x)
        d = jnp.where(step_y == 0, 1 + by_x, d)
        d = jnp.where(step_x == 0, jnp.where(step_y == 0, 0, 3 + by_y), d)
        s = taken[d]
        taken[d] = s + 1
        index[pl.ds(d * 16 + s, 1), :] = hi_all[e : e + 1, :]
        index[pl.ds(d * 16 + 8 + s, 1), :] = lo_all[e : e + 1, :]
        block = block_ref[e]
        feat = jnp.where(lane < counts_ref[block], feat_ref[block].astype(F32), 0.0).astype(BF)
        value = jnp.dot(feat, weight_ref[e], preferred_element_type=F32)
        start = pl.multiple_of(s * CHAN, CHAN)
        packed[d, pl.ds(start, CHAN), :] = value.astype(BF)
    copies = []
    for d in (1, 2, 3, 4, 5, 6, 7, 8, 0):
        packed[d, SLOTS * CHAN :, :] = index[d * 16 : d * 16 + 16, :].astype(BF)
        copies.append(pltpu.make_async_copy(packed.at[d], outs[d], sem.at[CHUNKS + 1 + d]))
        copies[-1].start()
    for c in copies:
        c.wait()


def group_size(rows):
    return 8 if rows is None else 4


def scatter_kernel(parts, first, rows, *refs):
    got = refs[:parts]
    refs = refs[parts:]
    if not first:
        before = refs[0]
        refs = refs[1:]
    if rows is None:
        acc, values, index, hi_all, lo_all = refs
        groups = list(range(16))
    else:
        grid_ref = refs[0]
        sides = refs[1:-5]
        values, index, hi_all, lo_all, acc = refs[-5:]
        groups = [4 * x + k for x in rows for k in range(4)]
    hi_all[...] = jnp.full(hi_all.shape, -1.0, F32)
    lo_all[...] = jnp.full(lo_all.shape, -1.0, F32)
    counts = []
    for d in range(parts):
        marks = got[d][SLOTS * CHAN :, :].astype(F32)
        index[d * 16 : d * 16 + 16, :] = marks
        counts.append(jnp.sum(jnp.where(marks[0:8, 0:1] >= 0.0, 1.0, 0.0)).astype(I32))
    filled = jnp.int32(0)
    for d in range(parts):

        def copy(s, pos, d=d):
            values[pos] = got[d][pl.ds(pl.multiple_of(s * CHAN, CHAN), CHAN), :]
            hi_all[pl.ds(pos, 1), :] = index[pl.ds(d * 16 + s, 1), :]
            lo_all[pl.ds(pos, 1), :] = index[pl.ds(d * 16 + 8 + s, 1), :]
            return pos + 1

        filled = lax.fori_loop(0, counts[d], copy, filled)
    row = lax.broadcasted_iota(I32, (256, LANES), 0).astype(F32)
    for i, t in enumerate(groups):
        piece = slice(i * CHAN, (i + 1) * CHAN)
        if first:
            acc[piece, :] = jnp.zeros((CHAN, 256), F32)
        else:
            acc[piece, :] = before[t * CHAN : (t + 1) * CHAN, :]

    size = group_size(rows)

    def step(g, carry):
        left = [[] for _ in groups]
        right = []
        for j in range(size):
            e = g * size + j
            value = values[e]
            hi = jnp.broadcast_to(hi_all[pl.ds(e, 1), :], (CHAN, LANES)).astype(BF)
            lo = lo_all[pl.ds(e, 1), :]
            right.append(jnp.where(row == lo, 1.0, 0.0).astype(BF))
            for kept, t in zip(left, groups):
                kept.append(jnp.where(hi == jnp.array(t, BF), value, jnp.array(0, BF)))
        a = jnp.concatenate([jnp.concatenate(kept, axis=1) for kept in left], axis=0)
        b = jnp.concatenate(right, axis=1)
        acc[...] += lax.dot_general(a, b, NT, preferred_element_type=F32)
        return carry

    lax.fori_loop(0, (filled + size - 1) // size, step, 0)
    if rows is None:
        return
    for i in range(len(groups)):
        for half in range(2):
            column = acc[i * CHAN : (i + 1) * CHAN, half * LANES : (half + 1) * LANES].astype(BF)
            grid_ref[i // 4, (i % 4) * 2 + half] = column
    if sides:
        in_order((lax.axis_index("gx") + 1) % 2, *sides, grid_ref.at[0], grid_ref.at[1])


def scatter(parts, before, rows=None):
    most = len(parts) * SLOTS + group_size(rows)
    sums = ((16 * CHAN, 256), F32)
    first = before is None
    if rows is None:
        outs = [sums]
        scratch = []
    else:
        outs = [((len(rows), TILE_Y, CHAN, LANES), BF)]
        if rows == OUTER:
            outs += [((TILE_Y, CHAN, LANES), BF)] * 2
        scratch = [pltpu.VMEM((len(rows) * 4 * CHAN, 256), F32)]
    return call(
        functools.partial(scatter_kernel, len(parts), first, rows),
        outs,
        [VM] * (len(parts) + (not first)),
        [
            pltpu.VMEM((most, CHAN, LANES), BF),
            pltpu.VMEM((len(parts) * 16, LANES), F32),
            pltpu.VMEM((most, LANES), F32),
            pltpu.VMEM((most, LANES), F32),
        ]
        + scratch,
        800000000,
    )(*parts, *([] if first else [before]))


def cell(outer_ref, middle_ref, x, y):
    return outer_ref[x // (TILE_X - 1), y] if x in OUTER else middle_ref[x - 1, y]


def shifted(column):
    lane = lax.broadcasted_iota(I32, column.shape, 1)
    wide = column.astype(F32)
    before = jnp.where(lane == 0, 0.0, pltpu.roll(wide, 1, 1)).astype(BF)
    after = jnp.where(lane == LANES - 1, 0.0, pltpu.roll(wide, LANES - 1, 1)).astype(BF)
    return jnp.concatenate([before, column, after], axis=0)


def conv_rows(picks, weight_ref, size_x, put):
    weight = weight_ref[...]
    sums = [None] * size_x
    for x in range(size_x + 2):
        rhs = jnp.concatenate(picks(x), axis=1)
        first = max(0, x - size_x + 1)
        last = min(2, x)
        prod = jnp.dot(weight[first * CHAN : (last + 1) * CHAN], rhs, preferred_element_type=F32)
        for a in range(first, last + 1):
            piece = prod[(a - first) * CHAN : (a - first + 1) * CHAN]
            out = x - a
            sums[out] = piece if sums[out] is None else sums[out] + piece
        if x >= 2:
            put(x - 2, sums[x - 2])
            sums[x - 2] = None


def flat(taps):
    return taps.reshape(9 * CHAN, LANES)


def silu(v):
    return v / (1.0 + jnp.exp(-v))


def edges():
    index_x = lax.axis_index("gx")
    index_y = lax.axis_index("gy")
    x_lo = index_x > 0
    x_hi = index_x < lax.axis_size("gx") - 1
    y_lo = index_y > 0
    y_hi = index_y < lax.axis_size("gy") - 1
    return x_lo, x_hi, y_lo, y_hi


def in_order(odd, one_ref, two_ref, low_ref, high_ref):
    @pl.when(odd == 0)
    def _():
        one_ref[...] = high_ref[...]
        two_ref[...] = low_ref[...]

    @pl.when(odd == 1)
    def _():
        one_ref[...] = low_ref[...]
        two_ref[...] = high_ref[...]


def sorted_x(one_ref, two_ref, xl_ref, xh_ref):
    x_lo, x_hi, _, _ = edges()
    odd = (lax.axis_index("gx") + 1) % 2 == 1
    for i in range(xl_ref.shape[0]):
        one = one_ref[i].astype(F32)
        two = two_ref[i].astype(F32)
        xl_ref[i] = jnp.where(x_lo, jnp.where(odd, one, two), 0.0).astype(BF)
        xh_ref[i] = jnp.where(x_hi, jnp.where(odd, two, one), 0.0).astype(BF)


def sorted_y(one_ref, two_ref, i):
    _, _, y_lo, y_hi = edges()
    odd = (lax.axis_index("gy") + 1) % 2 == 1
    one = one_ref[i].astype(F32)
    two = two_ref[i].astype(F32)
    lower = jnp.where(y_lo, jnp.where(odd, one, two), 0.0).astype(BF)
    higher = jnp.where(y_hi, jnp.where(odd, two, one), 0.0).astype(BF)
    return lower, higher


def grid_side_kernel(
    one_ref, two_ref, outer_ref, middle_ref, xl_ref, xh_ref, y_one_ref, y_two_ref, low, high
):
    sorted_x(one_ref, two_ref, xl_ref, xh_ref)
    for ref, y in ((low, 0), (high, TILE_Y - 1)):
        ref[0] = xl_ref[y]
        for x in range(TILE_X):
            ref[x + 1] = cell(outer_ref, middle_ref, x, y)
        ref[TILE_X + 1] = xh_ref[y]
    in_order((lax.axis_index("gy") + 1) % 2, y_one_ref, y_two_ref, low, high)


def coarse_side_kernel(
    one_ref, two_ref, coarse_ref, down_ref, up_ref,
    xl_ref, xh_ref, y_one_ref, y_two_ref, low, high,
):
    sorted_x(one_ref, two_ref, xl_ref, xh_ref)
    half_y = TILE_Y // 2
    left = xl_ref[8].astype(F32)
    right = xh_ref[8].astype(F32)
    for ref, y, own, row in ((low, 0, down_ref, 48), (high, half_y - 2, up_ref, 54)):
        for x in range(2):
            for k in range(2):
                ref[x * 2 + k] = xl_ref[x * half_y + y + k]
                ref[4 + x * 2 + k] = coarse_ref[x, y + k]
                ref[8 + x * 2 + k] = xh_ref[x * half_y + y + k]
        ref[12] = filled_up([own[...], left[row : row + 6], right[row : row + 6]])
    in_order((lax.axis_index("gy") + 1) % 2, y_one_ref, y_two_ref, low, high)


def field_side_kernel(one_ref, two_ref, own_ref, row_ref):
    odd = (lax.axis_index("gx") + 1) % 2
    row_ref[1] = own_ref[...]

    @pl.when(odd == 0)
    def _():
        row_ref[0] = two_ref[...]
        row_ref[2] = one_ref[...]

    @pl.when(odd == 1)
    def _():
        row_ref[0] = one_ref[...]
        row_ref[2] = two_ref[...]


def masked(column, *conditions):
    keep = functools.reduce(jnp.logical_and, conditions)
    return jnp.where(keep, column.astype(F32), 0.0).astype(BF)


def inner_conv_kernel(outer_ref, middle_ref, xl_ref, xh_ref, weight_ref, stack, act_ref):
    for y in range(TILE_Y):
        for x in range(TILE_X):
            stack[x + 1, y] = shifted(cell(outer_ref, middle_ref, x, y))
        stack[0, y] = shifted(xl_ref[y])
        stack[TILE_X + 1, y] = shifted(xh_ref[y])
    for y in range(1, TILE_Y - 1, 2):

        def picks(x, y=y):
            return [flat(stack[x, y - 1 : y + 2]), flat(stack[x, y : y + 3])]

        def put(x, value, y=y):
            for k in range(2):
                part = value[:, k * LANES : (k + 1) * LANES]
                own = cell(outer_ref, middle_ref, x, y + k).astype(F32)
                act_ref[x, y - 1 + k] = (silu(part) + own).astype(BF)

        conv_rows(picks, weight_ref, TILE_X, put)


def joined(total):
    lane = lax.broadcasted_iota(I32, (8, LANES), 1)
    before = jnp.where(lane == 0, 0.0, pltpu.roll(total[0:8], 1, 1))
    after = jnp.where(lane == LANES - 1, 0.0, pltpu.roll(total[16:24], LANES - 1, 1))
    both = before + total[8:16] + after
    return both[0:3] + both[3:6]


def two_parts(value):
    high = value.astype(BF).astype(F32)
    return jnp.concatenate([high, value - high], axis=0)


def filled_up(pieces):
    rest = CHAN - sum(piece.shape[0] for piece in pieces)
    return jnp.concatenate(pieces + [jnp.zeros((rest, LANES), F32)], axis=0).astype(BF)


def added(pieces):
    return functools.reduce(lambda one, two: one + two, pieces)


def outer_conv_kernel(
    outer_ref, middle_ref, stack, inner_ref, y_one_ref, y_two_ref, weight_ref, out_weight_ref,
    act_ref, coarse_ref, one_ref, two_ref, edge, taps, low_ref, high_ref,
):
    for x in range(TILE_X + 2):
        lower, higher = sorted_y(y_one_ref, y_two_ref, x)
        edge[x, 0] = shifted(lower)
        edge[x, 1] = shifted(higher)
    last_y = TILE_Y - 1

    def picks(x):
        return [
            jnp.concatenate([edge[x, 0], stack[x, 0], stack[x, 1]], axis=0),
            jnp.concatenate([stack[x, last_y - 1], stack[x, last_y], edge[x, 1]], axis=0),
        ]

    def put(x, value):
        for k, y in enumerate((0, last_y)):
            part = value[:, k * LANES : (k + 1) * LANES]
            own = cell(outer_ref, middle_ref, x, y).astype(F32)
            act_ref[x, y] = (silu(part) + own).astype(BF)

    conv_rows(picks, weight_ref, TILE_X, put)
    for x in range(TILE_X):
        for y in range(1, last_y):
            act_ref[x, y] = inner_ref[x, y - 1]
    half_y = TILE_Y // 2
    for x in range(TILE_X // 2):
        for y in range(half_y):
            total = (
                act_ref[2 * x, 2 * y].astype(F32)
                + act_ref[2 * x, 2 * y + 1].astype(F32)
                + act_ref[2 * x + 1, 2 * y].astype(F32)
                + act_ref[2 * x + 1, 2 * y + 1].astype(F32)
            )
            result = (total * 0.25).astype(BF)
            coarse_ref[x, y] = result
            low_ref[x * half_y + y] = result
            high_ref[x * half_y + y] = result
    for side, ref, x, a in ((0, low_ref, 0, 2), (1, high_ref, TILE_X - 1, 0)):
        weight = out_weight_ref[a * 72 : a * 72 + 80]
        for y in range(0, TILE_Y, 2):
            rhs = jnp.concatenate([act_ref[x, y], act_ref[x, y + 1]], axis=1)
            prod = jnp.dot(weight, rhs, preferred_element_type=F32)
            taps[side, y] = prod[:, :LANES]
            taps[side, y + 1] = prod[:, LANES:]
        cells = []
        for y in [*range(TILE_Y), -1, TILE_Y]:
            near = [(y + b - 1, b) for b in range(3) if 0 <= y + b - 1 < TILE_Y]
            total = added([taps[side, v, b * 24 : b * 24 + 24, :] for v, b in near])
            cells.append(two_parts(joined(total)))
        ref[8] = filled_up(cells)
    in_order((lax.axis_index("gx") + 1) % 2, one_ref, two_ref, low_ref, high_ref)


def rim_kernel(act_ref, out_weight_ref, down_ref, up_ref, taps):
    weight = out_weight_ref[...]
    for ref, y, b in ((down_ref, 0, 2), (up_ref, TILE_Y - 1, 0)):
        for x in range(0, TILE_X, 2):
            rhs = jnp.concatenate([act_ref[x, y], act_ref[x + 1, y]], axis=1)
            prod = jnp.dot(weight, rhs, preferred_element_type=F32)
            taps[x] = prod[:, :LANES]
            taps[x + 1] = prod[:, LANES:]
        cells = []
        for x in range(TILE_X):
            near = [(x + a - 1, (a * 3 + b) * 24) for a in range(3) if 0 <= x + a - 1 < TILE_X]
            total = added([taps[u, start : start + 24, :] for u, start in near])
            cells.append(two_parts(joined(total)))
        ref[...] = jnp.concatenate(cells, axis=0)


def put_taps(weight, taps, places, columns):
    for (one, two), pair in zip(zip(places[::2], places[1::2]), zip(columns[::2], columns[1::2])):
        prod = jnp.dot(weight, jnp.concatenate(pair, axis=1), preferred_element_type=F32)
        taps[one] = prod[:, :LANES]
        taps[two] = prod[:, LANES:]


def inner_mid_kernel(
    coarse_ref, xl_ref, xh_ref, act_ref, mid_weight_ref, out_weight_ref, stack, taps, mid_ref
):
    x_lo, x_hi, _, _ = edges()
    half_x = TILE_X // 2
    half_y = TILE_Y // 2
    for x in range(half_x):
        for y in range(half_y):
            stack[x + 2, y] = shifted(coarse_ref[x, y])
            stack[x, y] = shifted(xl_ref[x * half_y + y])
            stack[x + 2 + half_x, y] = shifted(xh_ref[x * half_y + y])

    def picks(x):
        return [flat(stack[x, 0:3]), flat(stack[x, 1:4])]

    def put(x, value):
        result = silu(value).astype(BF)
        mid_ref[x, 0] = result[:, :LANES]
        mid_ref[x, 1] = result[:, LANES:]

    conv_rows(picks, mid_weight_ref, half_x + 2, put)
    weight = out_weight_ref[...]
    for x in range(TILE_X + 2):
        columns = []
        for y in range(4):
            value = mid_ref[(x + 1) // 2, y // 2]
            if x == 0:
                columns.append(masked(value, x_lo))
            elif x == TILE_X + 1:
                columns.append(masked(value, x_hi))
            else:
                fine = act_ref[x - 1, y + 2].astype(F32)
                columns.append((fine + value.astype(F32)).astype(BF))
        put_taps(weight, taps, [(x, y) for y in range(4)], columns)


def outer_mid_kernel(
    act_ref, stack, inner, xl_ref, xh_ref, y_one_ref, y_two_ref, mid_weight_ref, out_weight_ref,
    field_ref, sent_ref, edge, mid_ref, taps, yl_ref, yh_ref,
):
    x_lo, x_hi, y_lo, y_hi = edges()
    half_x = TILE_X // 2
    for i in range(13):
        yl_ref[i], yh_ref[i] = sorted_y(y_one_ref, y_two_ref, i)
    for x in range(half_x + 4):
        for k in range(2):
            edge[x, k] = shifted(yl_ref[x * 2 + k])
            edge[x, 2 + k] = shifted(yh_ref[x * 2 + k])
    for side in range(2):

        def picks(x, side=side):
            if side == 0:
                near = [edge[x, 0], edge[x, 1], stack[x, 0], stack[x, 1]]
            else:
                near = [stack[x, 2], stack[x, 3], edge[x, 2], edge[x, 3]]
            return [jnp.concatenate(near[:3], axis=0), jnp.concatenate(near[1:], axis=0)]

        def put(x, value, side=side):
            result = silu(value).astype(BF)
            mid_ref[x, 2 * side] = result[:, :LANES]
            mid_ref[x, 2 * side + 1] = result[:, LANES:]

        conv_rows(picks, mid_weight_ref, half_x + 2, put)
    weight = out_weight_ref[...]
    rows = (-1, 0, 1, TILE_Y - 2, TILE_Y - 1, TILE_Y)
    for x in range(TILE_X + 2):
        columns = []
        for y, k in zip(rows, (0, 1, 1, 2, 2, 3)):
            value = mid_ref[(x + 1) // 2, k]
            more = ()
            if x == 0:
                more += (x_lo,)
            if x == TILE_X + 1:
                more += (x_hi,)
            if y < 0:
                more += (y_lo,)
            if y == TILE_Y:
                more += (y_hi,)
            if more:
                columns.append(masked(value, *more))
            else:
                fine = act_ref[x - 1, y].astype(F32)
                columns.append((fine + value.astype(F32)).astype(BF))
        put_taps(weight, taps, [(x, k) for k in range(6)], columns)

    def tap(x, y, start):
        if y in rows:
            return taps[x, rows.index(y), start : start + 24, :]
        return inner[x, y - 2, start : start + 24, :]

    def received(ref, place, row):
        piece = ref[place].astype(F32)[row : row + 6]
        return piece[0:3] + piece[3:6]

    for x in range(TILE_X):
        for y in range(TILE_Y):
            value = joined(
                added(
                    [
                        tap(x + a, y + b - 1, (a * 3 + b) * 24)
                        for a in range(3)
                        for b in range(3)
                    ]
                )
            )
            x_ref = xl_ref if x == 0 else xh_ref
            y_ref = yl_ref if y == 0 else yh_ref
            on_x = x in (0, TILE_X - 1)
            on_y = y in (0, TILE_Y - 1)
            if on_x:
                value += received(x_ref, 8, y * 6)
            if on_y:
                value += received(y_ref, 12, x * 6)
            if on_x and on_y:
                value += received(y_ref, 12, 24 if x == 0 else 30)
            for d in range(3):
                field_ref[d, x * TILE_Y + y : x * TILE_Y + y + 1, :] = value[d : d + 1]
    sent_ref[...] = field_ref[...].astype(BF)


def gather_kernel(
    counts_ref, block_ref, dest_ref, own_ref, row_ref, y_two_ref, y_one_ref,
    nodes_ref, weight_ref, out_ref, frame, total,
):
    entries = weight_ref.shape[0]
    blocks = out_ref.shape[0]
    odd = (lax.axis_index("gy") + 1) % 2 == 1
    frame[5] = own_ref[...]
    for i in range(3):
        one = y_one_ref[i].astype(F32)
        two = y_two_ref[i].astype(F32)
        frame[3 * i + 1] = jnp.where(odd, one, two)
        frame[3 * i + 3] = jnp.where(odd, two, one)
        if i != 1:
            frame[3 * i + 2] = row_ref[i].astype(F32)
    total[...] = jnp.zeros(total.shape, F32)
    sub = lax.broadcasted_iota(I32, (8, LANES), 0)
    for e in range(entries):
        tile = dest_ref[e]
        d = (tile // lax.axis_size("gy") - lax.axis_index("gx") + 1) * 3 + (tile % lax.axis_size("gy") - lax.axis_index("gy") + 1)
        node = jnp.broadcast_to(nodes_ref[e : e + 1, :], (8, LANES))
        z = node & (LANES - 1)
        column = node >> 7
        rows = []
        for c in range(3):
            picked = None
            for q in range(4):
                table = frame[d + 1, c, q * 8 : q * 8 + 8, :]
                value = jnp.take_along_axis(table, z, axis=1)
                value = jnp.where(column == sub + q * 8, value, 0.0)
                picked = value if picked is None else picked + value
            rows.append(picked)
        wide = jnp.concatenate(rows, axis=0)
        high = wide.astype(BF)
        low = (wide - high.astype(F32)).astype(BF)
        both = jnp.concatenate([high, low], axis=0)
        value = lax.dot_general(both, weight_ref[e], NT, preferred_element_type=F32)
        block = block_ref[e]
        total[block] += value[0:24] + value[24:48]
    lane = lax.broadcasted_iota(I32, (1, LANES), 1)
    for b in range(blocks):
        live = lane < counts_ref[b]
        for c in range(3):
            value = jnp.sum(total[b, c * 8 : c * 8 + 8, :], axis=0, keepdims=True)
            out_ref[b, c : c + 1, :] = jnp.where(live, value, 0.0)


def partners(size_x, size_y, step_x, step_y, parity):
    left = [(0, y) for y in range(size_y)]
    top = [(x, size_y - 1) for x in range(1, size_x)]
    right = [(size_x - 1, y) for y in reversed(range(size_y - 1))]
    bottom = [(x, 0) for x in reversed(range(1, size_x - 1))]
    rim = left + top + right + bottom
    if not step_x:
        rim = rim[size_y - 1 :] + rim[: size_y - 1]
    partner = {}
    for x in range(size_x):
        for y in range(size_y):
            sign = 1 if (x if step_x else y) % 2 == parity else -1
            to = (x + sign * step_x, y + sign * step_y)
            if 0 <= to[0] < size_x and 0 <= to[1] < size_y:
                partner[x, y] = to
    alone = [place for place in rim if place not in partner]
    for one, two in zip(alone[::2], alone[1::2]):
        partner[one] = two
        partner[two] = one
    return partner


def swapped(value, step_x, step_y, parity):
    size_x = lax.axis_size("gx")
    size_y = lax.axis_size("gy")
    partner = partners(size_x, size_y, step_x, step_y, parity)
    pairs = [
        (x * size_y + y, to_x * size_y + to_y) for (x, y), (to_x, to_y) in sorted(partner.items())
    ]
    return lax.ppermute(value, ("gx", "gy"), pairs)


def across_x(one, two):
    return swapped(one, 1, 0, 1), swapped(two, 1, 0, 0)


def across_y(one, two):
    return swapped(one, 0, 1, 1), swapped(two, 0, 1, 0)


def shards(
    particle_feat, block_counts, entry_block, entry_dest, entry_nodes, entry_weights,
    conv_in, conv_mid, conv_out, head_weight,
):
    blocks = particle_feat.shape[0]
    entries = entry_weights.shape[0]
    dest = entry_dest.reshape(entries)
    in_weight = conv_in.reshape(3 * CHAN, 9 * CHAN)
    mid_weight = conv_mid.reshape(3 * CHAN, 9 * CHAN)
    folded = jnp.einsum(
        "do,aox->adx", head_weight, conv_out.astype(F32), precision=lax.Precision.HIGHEST
    )
    high = lax.reduce_precision(folded, 8, 7)
    both = jnp.concatenate([high, folded - high, jnp.zeros((3, 2, 9 * CHAN), F32)], axis=1)
    out_weight = (
        both.reshape(3, 8, 9, CHAN).transpose(0, 2, 1, 3).reshape(27 * 8, CHAN).astype(BF)
    )
    out_weight = jnp.pad(out_weight, ((0, PADDED - 27 * 8), (0, 0)))

    packed = (SLOTS * CHAN + 16, LANES)
    sent = call(
        partial_kernel,
        [(packed, BF)] * 9,
        [SM] * 3 + [HB, VM, HB],
        [
            pltpu.VMEM(particle_feat.shape, BF),
            pltpu.VMEM(entry_weights.shape, BF),
            pltpu.SemaphoreType.DMA((CHUNKS + 10,)),
            pltpu.VMEM((9, *packed), BF),
            pltpu.VMEM((entries, LANES), F32),
            pltpu.VMEM((entries, LANES), F32),
            pltpu.VMEM((9 * 16, LANES), F32),
            pltpu.SMEM((9,), I32),
        ],
        70000000,
        limit=60 * 1024 * 1024,
        to=HB,
    )(block_counts, entry_block, dest, particle_feat, entry_nodes, entry_weights)
    sides = [*across_x(sent[1], sent[2]), *across_y(sent[3], sent[4])]
    sums = scatter([sent[0]], None)[0]
    corners = sent[5:]
    corners = [
        swapped(value, 1, 1 - 2 * (i // 2), 1 - i % 2) for i, value in enumerate(corners)
    ]
    sums = scatter([*sides, *corners[:2]], sums)[0]
    outer, one, two = scatter(corners[2:], sums, OUTER)
    middle = scatter(corners[2:], sums, MIDDLE)[0]

    column = (CHAN, LANES)
    one, two = across_x(one, two)
    xl, xh, one, two = call(
        grid_side_kernel,
        [((TILE_Y, *column), BF)] * 2 + [((TILE_X + 2, *column), BF)] * 2,
        [VM] * 4,
        [pltpu.VMEM((TILE_X + 2, *column), BF)] * 2,
        1000000,
    )(one, two, outer, middle)
    one, two = across_y(one, two)
    stack, inner = call(
        inner_conv_kernel,
        [
            ((TILE_X + 2, TILE_Y, 3 * CHAN, LANES), BF),
            ((TILE_X, TILE_Y - 2, CHAN, LANES), BF),
        ],
        [VM] * 5,
        [],
        1000000000,
    )(outer, middle, xl, xh, in_weight)
    act, coarse, one, two = call(
        outer_conv_kernel,
        [
            ((TILE_X, TILE_Y, *column), BF),
            ((TILE_X // 2, TILE_Y // 2, *column), BF),
            ((9, *column), BF),
            ((9, *column), BF),
        ],
        [VM] * 8,
        [
            pltpu.VMEM((TILE_X + 2, 2, 3 * CHAN, LANES), BF),
            pltpu.VMEM((2, TILE_Y, 80, LANES), F32),
            pltpu.VMEM((9, *column), BF),
            pltpu.VMEM((9, *column), BF),
        ],
        600000000,
    )(outer, middle, stack, inner, one, two, in_weight, out_weight)

    one, two = across_x(one, two)
    down, up = call(
        rim_kernel,
        [((24, LANES), F32)] * 2,
        [VM] * 2,
        [pltpu.VMEM((TILE_X, PADDED, LANES), F32)],
        1000000000,
    )(act, out_weight)
    xl, xh, one, two = call(
        coarse_side_kernel,
        [((9, *column), BF)] * 2 + [((13, *column), BF)] * 2,
        [VM] * 5,
        [pltpu.VMEM((13, *column), BF)] * 2,
        1000000,
    )(one, two, coarse, down, up)
    one, two = across_y(one, two)
    stack, inner = call(
        inner_mid_kernel,
        [
            ((6, TILE_Y // 2, 3 * CHAN, LANES), BF),
            ((TILE_X + 2, 4, PADDED, LANES), F32),
        ],
        [VM] * 6,
        [pltpu.VMEM((4, 2, *column), BF)],
        1000000000,
    )(coarse, xl, xh, act, mid_weight, out_weight)
    field, rounded = call(
        outer_mid_kernel,
        [((3, TILE_X * TILE_Y, LANES), F32), ((3, TILE_X * TILE_Y, LANES), BF)],
        [VM] * 9,
        [
            pltpu.VMEM((6, 4, 3 * CHAN, LANES), BF),
            pltpu.VMEM((4, 4, *column), BF),
            pltpu.VMEM((TILE_X + 2, 6, PADDED, LANES), F32),
            pltpu.VMEM((13, *column), BF),
            pltpu.VMEM((13, *column), BF),
        ],
        1300000000,
    )(act, stack, inner, xl, xh, one, two, mid_weight, out_weight)

    one, two = across_x(rounded, rounded)
    row = call(
        field_side_kernel,
        [((3, 3, TILE_X * TILE_Y, LANES), BF)],
        [VM] * 3,
        [],
        1000000,
    )(one, two, rounded)[0]
    one, two = across_y(row, row)
    return call(
        gather_kernel,
        [((blocks, 3, LANES), F32)],
        [SM] * 3 + [VM] * 6,
        [
            pltpu.VMEM((10, 3, TILE_X * TILE_Y, LANES), F32),
            pltpu.VMEM((blocks, 24, LANES), F32),
        ],
        70000000,
    )(
        block_counts, entry_block, dest, field, row, two, one, entry_nodes, entry_weights
    )[0]


def solution(mesh):
    in_specs = (
        P(("gx", "gy"), None, None),
        P(("gx", "gy")),
        P(("gx", "gy")),
        P(("gx", "gy"), None),
        P(("gx", "gy"), None),
        P(("gx", "gy"), None, None),
        P(),
        P(),
        P(),
        P(),
    )
    out_specs = P(("gx", "gy"), None, None)
    return jax.shard_map(shards, mesh=mesh, in_specs=in_specs, out_specs=out_specs, check_vma=False)
```

```python
import functools

import jax
import jax.numpy as jnp
from jax import lax
from jax.experimental import pallas as pl
from jax.experimental.pallas import tpu as pltpu
from jax.sharding import PartitionSpec as P

BF = jnp.bfloat16
F32 = jnp.float32
I32 = jnp.int32

CHAN = 64
LANES = 128
TILE_X = 4
TILE_Y = 8
SLOTS = 8
CHUNKS = 4
PADDED = 224
OUTER = (0, TILE_X - 1)
MIDDLE = tuple(range(1, TILE_X - 1))
VMEM_LIMIT = 40 * 1024 * 1024

VM = pl.BlockSpec(memory_space=pltpu.VMEM)
SM = pl.BlockSpec(memory_space=pltpu.SMEM)
HB = pl.BlockSpec(memory_space=pltpu.HBM)
NT = (((1,), (1,)), ((), ()))


def call(kernel, outs, ins, scratch, flops, limit=VMEM_LIMIT, to=VM):
    return pl.pallas_call(
        kernel,
        out_shape=[jax.ShapeDtypeStruct(s, d) for s, d in outs],
        in_specs=ins,
        out_specs=[to] * len(outs),
        scratch_shapes=scratch,
        compiler_params=pltpu.CompilerParams(vmem_limit_bytes=limit),
        cost_estimate=pl.CostEstimate(flops=flops, bytes_accessed=2000000, transcendentals=0),
    )


def partial_kernel(
    counts_ref, block_ref, dest_ref, feat_hbm, nodes_ref, weight_hbm, *rest
):
    outs = rest[:9]
    feat_ref, weight_ref, sem, packed, hi_all, lo_all, index, taken = rest[9:]
    entries = weight_ref.shape[0]
    size = entries // CHUNKS
    copies = [pltpu.make_async_copy(feat_hbm, feat_ref, sem.at[CHUNKS])]
    for c in range(CHUNKS):
        rows = pl.ds(c * size, size)
        copies.append(pltpu.make_async_copy(weight_hbm.at[rows], weight_ref.at[rows], sem.at[c]))
    for c in copies:
        c.start()
    nodes = nodes_ref[...]
    hi_all[...] = (nodes >> 8).astype(F32)
    lo_all[...] = (nodes & 255).astype(F32)
    index[...] = jnp.full(index.shape, -1.0, F32)
    for d in range(9):
        taken[d] = 0
    index_x = lax.axis_index("gx")
    index_y = lax.axis_index("gy")
    odd_x = (index_x + 1) % 2
    odd_y = (index_y + 1) % 2
    lane = lax.broadcasted_iota(I32, (CHAN, LANES), 1)
    copies[0].wait()
    for e in range(entries):
        if e % size == 0:
            copies[1 + e // size].wait()
        tile = dest_ref[e]
        step_x = tile // lax.axis_size("gy") - index_x
        step_y = tile % lax.axis_size("gy") - index_y
        by_x = jnp.where(step_x > 0, odd_x, 1 - odd_x)
        by_y = jnp.where(step_y > 0, odd_y, 1 - odd_y)
        d = jnp.where(step_x == step_y, 5 + by_x, 7 + by_x)
        d = jnp.where(step_y == 0, 1 + by_x, d)
        d = jnp.where(step_x == 0, jnp.where(step_y == 0, 0, 3 + by_y), d)
        s = taken[d]
        taken[d] = s + 1
        index[pl.ds(d * 16 + s, 1), :] = hi_all[e : e + 1, :]
        index[pl.ds(d * 16 + 8 + s, 1), :] = lo_all[e : e + 1, :]
        block = block_ref[e]
        feat = jnp.where(lane < counts_ref[block], feat_ref[block].astype(F32), 0.0).astype(BF)
        value = jnp.dot(feat, weight_ref[e], preferred_element_type=F32)
        start = pl.multiple_of(s * CHAN, CHAN)
        packed[d, pl.ds(start, CHAN), :] = value.astype(BF)
    copies = []
    for d in (1, 2, 3, 4, 5, 6, 7, 8, 0):
        packed[d, SLOTS * CHAN :, :] = index[d * 16 : d * 16 + 16, :].astype(BF)
        copies.append(pltpu.make_async_copy(packed.at[d], outs[d], sem.at[CHUNKS + 1 + d]))
        copies[-1].start()
    for c in copies:
        c.wait()


def group_size(rows):
    return 8 if rows is None else 4


def scatter_kernel(parts, first, rows, *refs):
    got = refs[:parts]
    refs = refs[parts:]
    if not first:
        before = refs[0]
        refs = refs[1:]
    if rows is None:
        acc, values, index, hi_all, lo_all = refs
        groups = list(range(16))
    else:
        grid_ref = refs[0]
        sides = refs[1:-5]
        values, index, hi_all, lo_all, acc = refs[-5:]
        groups = [4 * x + k for x in rows for k in range(4)]
    hi_all[...] = jnp.full(hi_all.shape, -1.0, F32)
    lo_all[...] = jnp.full(lo_all.shape, -1.0, F32)
    counts = []
    for d in range(parts):
        marks = got[d][SLOTS * CHAN :, :].astype(F32)
        index[d * 16 : d * 16 + 16, :] = marks
        counts.append(jnp.sum(jnp.where(marks[0:8, 0:1] >= 0.0, 1.0, 0.0)).astype(I32))
    filled = jnp.int32(0)
    for d in range(parts):

        def copy(s, pos, d=d):
            values[pos] = got[d][pl.ds(pl.multiple_of(s * CHAN, CHAN), CHAN), :]
            hi_all[pl.ds(pos, 1), :] = index[pl.ds(d * 16 + s, 1), :]
            lo_all[pl.ds(pos, 1), :] = index[pl.ds(d * 16 + 8 + s, 1), :]
            return pos + 1

        filled = lax.fori_loop(0, counts[d], copy, filled)
    row = lax.broadcasted_iota(I32, (256, LANES), 0).astype(F32)
    for i, t in enumerate(groups):
        piece = slice(i * CHAN, (i + 1) * CHAN)
        if first:
            acc[piece, :] = jnp.zeros((CHAN, 256), F32)
        else:
            acc[piece, :] = before[t * CHAN : (t + 1) * CHAN, :]

    size = group_size(rows)

    def step(g, carry):
        left = [[] for _ in groups]
        right = []
        for j in range(size):
            e = g * size + j
            value = values[e]
            hi = jnp.broadcast_to(hi_all[pl.ds(e, 1), :], (CHAN, LANES)).astype(BF)
            lo = lo_all[pl.ds(e, 1), :]
            right.append(jnp.where(row == lo, 1.0, 0.0).astype(BF))
            for kept, t in zip(left, groups):
                kept.append(jnp.where(hi == jnp.array(t, BF), value, jnp.array(0, BF)))
        a = jnp.concatenate([jnp.concatenate(kept, axis=1) for kept in left], axis=0)
        b = jnp.concatenate(right, axis=1)
        acc[...] += lax.dot_general(a, b, NT, preferred_element_type=F32)
        return carry

    lax.fori_loop(0, (filled + size - 1) // size, step, 0)
    if rows is None:
        return
    for i in range(len(groups)):
        for half in range(2):
            column = acc[i * CHAN : (i + 1) * CHAN, half * LANES : (half + 1) * LANES].astype(BF)
            grid_ref[i // 4, (i % 4) * 2 + half] = column
    if sides:
        in_order((lax.axis_index("gx") + 1) % 2, *sides, grid_ref.at[0], grid_ref.at[1])


def scatter(parts, before, rows=None):
    most = len(parts) * SLOTS + group_size(rows)
    sums = ((16 * CHAN, 256), F32)
    first = before is None
    if rows is None:
        outs = [sums]
        scratch = []
    else:
        outs = [((len(rows), TILE_Y, CHAN, LANES), BF)]
        if rows == OUTER:
            outs += [((TILE_Y, CHAN, LANES), BF)] * 2
        scratch = [pltpu.VMEM((len(rows) * 4 * CHAN, 256), F32)]
    return call(
        functools.partial(scatter_kernel, len(parts), first, rows),
        outs,
        [VM] * (len(parts) + (not first)),
        [
            pltpu.VMEM((most, CHAN, LANES), BF),
            pltpu.VMEM((len(parts) * 16, LANES), F32),
            pltpu.VMEM((most, LANES), F32),
            pltpu.VMEM((most, LANES), F32),
        ]
        + scratch,
        800000000,
    )(*parts, *([] if first else [before]))


def cell(outer_ref, middle_ref, x, y):
    return outer_ref[x // (TILE_X - 1), y] if x in OUTER else middle_ref[x - 1, y]


def shifted(column):
    lane = lax.broadcasted_iota(I32, column.shape, 1)
    wide = column.astype(F32)
    before = jnp.where(lane == 0, 0.0, pltpu.roll(wide, 1, 1)).astype(BF)
    after = jnp.where(lane == LANES - 1, 0.0, pltpu.roll(wide, LANES - 1, 1)).astype(BF)
    return jnp.concatenate([before, column, after], axis=0)


def conv_rows(picks, weight_ref, size_x, put):
    weight = weight_ref[...]
    sums = [None] * size_x
    for x in range(size_x + 2):
        rhs = jnp.concatenate(picks(x), axis=1)
        first = max(0, x - size_x + 1)
        last = min(2, x)
        prod = jnp.dot(weight[first * CHAN : (last + 1) * CHAN], rhs, preferred_element_type=F32)
        for a in range(first, last + 1):
            piece = prod[(a - first) * CHAN : (a - first + 1) * CHAN]
            out = x - a
            sums[out] = piece if sums[out] is None else sums[out] + piece
        if x >= 2:
            put(x - 2, sums[x - 2])
            sums[x - 2] = None


def flat(taps):
    return taps.reshape(9 * CHAN, LANES)


def silu(v):
    return v / (1.0 + jnp.exp(-v))


def edges():
    index_x = lax.axis_index("gx")
    index_y = lax.axis_index("gy")
    x_lo = index_x > 0
    x_hi = index_x < lax.axis_size("gx") - 1
    y_lo = index_y > 0
    y_hi = index_y < lax.axis_size("gy") - 1
    return x_lo, x_hi, y_lo, y_hi


def in_order(odd, one_ref, two_ref, low_ref, high_ref):
    @pl.when(odd == 0)
    def _():
        one_ref[...] = high_ref[...]
        two_ref[...] = low_ref[...]

    @pl.when(odd == 1)
    def _():
        one_ref[...] = low_ref[...]
        two_ref[...] = high_ref[...]


def sorted_x(one_ref, two_ref, xl_ref, xh_ref):
    x_lo, x_hi, _, _ = edges()
    odd = (lax.axis_index("gx") + 1) % 2 == 1
    zero = jnp.zeros((CHAN, LANES), BF)
    for i in range(xl_ref.shape[0]):
        one = one_ref[i]
        two = two_ref[i]
        xl_ref[i] = jnp.where(x_lo, jnp.where(odd, one, two), zero)
        xh_ref[i] = jnp.where(x_hi, jnp.where(odd, two, one), zero)


def sorted_y(one_ref, two_ref, i):
    _, _, y_lo, y_hi = edges()
    odd = (lax.axis_index("gy") + 1) % 2 == 1
    zero = jnp.zeros((CHAN, LANES), BF)
    one = one_ref[i]
    two = two_ref[i]
    lower = jnp.where(y_lo, jnp.where(odd, one, two), zero)
    higher = jnp.where(y_hi, jnp.where(odd, two, one), zero)
    return lower, higher


def grid_side_kernel(
    one_ref, two_ref, outer_ref, middle_ref, xl_ref, xh_ref, y_one_ref, y_two_ref, low, high
):
    sorted_x(one_ref, two_ref, xl_ref, xh_ref)
    for ref, y in ((low, 0), (high, TILE_Y - 1)):
        ref[0] = xl_ref[y]
        for x in range(TILE_X):
            ref[x + 1] = cell(outer_ref, middle_ref, x, y)
        ref[TILE_X + 1] = xh_ref[y]
    in_order((lax.axis_index("gy") + 1) % 2, y_one_ref, y_two_ref, low, high)


def coarse_side_kernel(
    one_ref, two_ref, coarse_ref, down_ref, up_ref,
    xl_ref, xh_ref, y_one_ref, y_two_ref, low, high,
):
    sorted_x(one_ref, two_ref, xl_ref, xh_ref)
    half_y = TILE_Y // 2
    left = xl_ref[8].astype(F32)
    right = xh_ref[8].astype(F32)
    for ref, y, own, row in ((low, 0, down_ref, 48), (high, half_y - 2, up_ref, 54)):
        for x in range(2):
            for k in range(2):
                ref[x * 2 + k] = xl_ref[x * half_y + y + k]
                ref[4 + x * 2 + k] = coarse_ref[x, y + k]
                ref[8 + x * 2 + k] = xh_ref[x * half_y + y + k]
        ref[12] = filled_up([own[...], left[row : row + 6], right[row : row + 6]])
    in_order((lax.axis_index("gy") + 1) % 2, y_one_ref, y_two_ref, low, high)


def field_side_kernel(one_ref, two_ref, own_ref, row_ref):
    odd = (lax.axis_index("gx") + 1) % 2
    row_ref[1] = own_ref[...]

    @pl.when(odd == 0)
    def _():
        row_ref[0] = two_ref[...]
        row_ref[2] = one_ref[...]

    @pl.when(odd == 1)
    def _():
        row_ref[0] = one_ref[...]
        row_ref[2] = two_ref[...]


def masked(column, *conditions):
    keep = functools.reduce(jnp.logical_and, conditions)
    return jnp.where(keep, column.astype(F32), 0.0).astype(BF)


def inner_conv_kernel(outer_ref, middle_ref, xl_ref, xh_ref, weight_ref, stack, act_ref):
    for y in range(TILE_Y):
        for x in range(TILE_X):
            stack[x + 1, y] = shifted(cell(outer_ref, middle_ref, x, y))
        stack[0, y] = shifted(xl_ref[y])
        stack[TILE_X + 1, y] = shifted(xh_ref[y])
    for y in range(1, TILE_Y - 1, 2):

        def picks(x, y=y):
            return [flat(stack[x, y - 1 : y + 2]), flat(stack[x, y : y + 3])]

        def put(x, value, y=y):
            for k in range(2):
                part = value[:, k * LANES : (k + 1) * LANES]
                own = cell(outer_ref, middle_ref, x, y + k).astype(F32)
                act_ref[x, y - 1 + k] = (silu(part) + own).astype(BF)

        conv_rows(picks, weight_ref, TILE_X, put)


def joined(total):
    lane = lax.broadcasted_iota(I32, (8, LANES), 1)
    before = jnp.where(lane == 0, 0.0, pltpu.roll(total[0:8], 1, 1))
    after = jnp.where(lane == LANES - 1, 0.0, pltpu.roll(total[16:24], LANES - 1, 1))
    both = before + total[8:16] + after
    return both[0:3] + both[3:6]


def two_parts(value):
    high = value.astype(BF).astype(F32)
    return jnp.concatenate([high, value - high], axis=0)


def filled_up(pieces):
    rest = CHAN - sum(piece.shape[0] for piece in pieces)
    return jnp.concatenate(pieces + [jnp.zeros((rest, LANES), F32)], axis=0).astype(BF)


def added(pieces):
    return functools.reduce(lambda one, two: one + two, pieces)


def outer_conv_kernel(
    outer_ref, middle_ref, stack, inner_ref, y_one_ref, y_two_ref, weight_ref, out_weight_ref,
    act_ref, coarse_ref, one_ref, two_ref, edge, taps, low_ref, high_ref,
):
    for x in range(TILE_X + 2):
        lower, higher = sorted_y(y_one_ref, y_two_ref, x)
        edge[x, 0] = shifted(lower)
        edge[x, 1] = shifted(higher)
    last_y = TILE_Y - 1

    def picks(x):
        return [
            jnp.concatenate([edge[x, 0], stack[x, 0], stack[x, 1]], axis=0),
            jnp.concatenate([stack[x, last_y - 1], stack[x, last_y], edge[x, 1]], axis=0),
        ]

    def put(x, value):
        for k, y in enumerate((0, last_y)):
            part = value[:, k * LANES : (k + 1) * LANES]
            own = cell(outer_ref, middle_ref, x, y).astype(F32)
            act_ref[x, y] = (silu(part) + own).astype(BF)

    conv_rows(picks, weight_ref, TILE_X, put)
    for x in range(TILE_X):
        for y in range(1, last_y):
            act_ref[x, y] = inner_ref[x, y - 1]
    half_y = TILE_Y // 2
    for x in range(TILE_X // 2):
        for y in range(half_y):
            total = (
                act_ref[2 * x, 2 * y].astype(F32)
                + act_ref[2 * x, 2 * y + 1].astype(F32)
                + act_ref[2 * x + 1, 2 * y].astype(F32)
                + act_ref[2 * x + 1, 2 * y + 1].astype(F32)
            )
            result = (total * 0.25).astype(BF)
            coarse_ref[x, y] = result
            low_ref[x * half_y + y] = result
            high_ref[x * half_y + y] = result
    for side, ref, x, a in ((0, low_ref, 0, 2), (1, high_ref, TILE_X - 1, 0)):
        weight = out_weight_ref[a * 72 : a * 72 + 80]
        for y in range(0, TILE_Y, 2):
            rhs = jnp.concatenate([act_ref[x, y], act_ref[x, y + 1]], axis=1)
            prod = jnp.dot(weight, rhs, preferred_element_type=F32)
            taps[side, y] = prod[:, :LANES]
            taps[side, y + 1] = prod[:, LANES:]
        cells = []
        for y in [*range(TILE_Y), -1, TILE_Y]:
            near = [(y + b - 1, b) for b in range(3) if 0 <= y + b - 1 < TILE_Y]
            total = added([taps[side, v, b * 24 : b * 24 + 24, :] for v, b in near])
            cells.append(two_parts(joined(total)))
        ref[8] = filled_up(cells)
    in_order((lax.axis_index("gx") + 1) % 2, one_ref, two_ref, low_ref, high_ref)


def rim_kernel(act_ref, out_weight_ref, down_ref, up_ref, taps):
    weight = out_weight_ref[...]
    for ref, y, b in ((down_ref, 0, 2), (up_ref, TILE_Y - 1, 0)):
        for x in range(0, TILE_X, 2):
            rhs = jnp.concatenate([act_ref[x, y], act_ref[x + 1, y]], axis=1)
            prod = jnp.dot(weight, rhs, preferred_element_type=F32)
            taps[x] = prod[:, :LANES]
            taps[x + 1] = prod[:, LANES:]
        cells = []
        for x in range(TILE_X):
            near = [(x + a - 1, (a * 3 + b) * 24) for a in range(3) if 0 <= x + a - 1 < TILE_X]
            total = added([taps[u, start : start + 24, :] for u, start in near])
            cells.append(two_parts(joined(total)))
        ref[...] = jnp.concatenate(cells, axis=0)


def put_taps(weight, taps, places, columns):
    for (one, two), pair in zip(zip(places[::2], places[1::2]), zip(columns[::2], columns[1::2])):
        prod = jnp.dot(weight, jnp.concatenate(pair, axis=1), preferred_element_type=F32)
        taps[one] = prod[:, :LANES]
        taps[two] = prod[:, LANES:]


def inner_mid_kernel(
    coarse_ref, xl_ref, xh_ref, act_ref, mid_weight_ref, out_weight_ref, stack, share, taps, mid_ref
):
    x_lo, x_hi, _, _ = edges()
    half_x = TILE_X // 2
    half_y = TILE_Y // 2
    for x in range(half_x):
        for y in range(half_y):
            stack[x + 2, y] = shifted(coarse_ref[x, y])
            stack[x, y] = shifted(xl_ref[x * half_y + y])
            stack[x + 2 + half_x, y] = shifted(xh_ref[x * half_y + y])

    def picks(x):
        return [flat(stack[x, 0:3]), flat(stack[x, 1:4])]

    def put(x, value):
        result = silu(value).astype(BF)
        mid_ref[x, 0] = result[:, :LANES]
        mid_ref[x, 1] = result[:, LANES:]

    conv_rows(picks, mid_weight_ref, half_x + 2, put)
    weight = out_weight_ref[...]
    for x in range(TILE_X + 2):
        columns = []
        for y in range(4):
            value = mid_ref[(x + 1) // 2, y // 2]
            if x == 0:
                columns.append(masked(value, x_lo))
            elif x == TILE_X + 1:
                columns.append(masked(value, x_hi))
            else:
                fine = act_ref[x - 1, y + 2].astype(F32)
                columns.append((fine + value.astype(F32)).astype(BF))
        put_taps(weight, taps, [(x, y) for y in range(4)], columns)
    for x in range(TILE_X):
        for y in range(1, TILE_Y - 1):
            near = [(a, b) for a in range(3) for b in range(3) if 2 <= y + b - 1 < 6]
            starts = [(x + a, y + b - 3, (a * 3 + b) * 24) for a, b in near]
            share[x, y - 1] = added([taps[u, v, i : i + 24, :] for u, v, i in starts])


def outer_mid_kernel(
    act_ref, stack, share_ref, xl_ref, xh_ref, y_one_ref, y_two_ref, mid_weight_ref, out_weight_ref,
    field_ref, sent_ref, edge, mid_ref, taps, yl_ref, yh_ref,
):
    x_lo, x_hi, y_lo, y_hi = edges()
    half_x = TILE_X // 2
    for i in range(13):
        yl_ref[i], yh_ref[i] = sorted_y(y_one_ref, y_two_ref, i)
    for x in range(half_x + 4):
        for k in range(2):
            edge[x, k] = shifted(yl_ref[x * 2 + k])
            edge[x, 2 + k] = shifted(yh_ref[x * 2 + k])
    for side in range(2):

        def picks(x, side=side):
            if side == 0:
                near = [edge[x, 0], edge[x, 1], stack[x, 0], stack[x, 1]]
            else:
                near = [stack[x, 2], stack[x, 3], edge[x, 2], edge[x, 3]]
            return [jnp.concatenate(near[:3], axis=0), jnp.concatenate(near[1:], axis=0)]

        def put(x, value, side=side):
            result = silu(value).astype(BF)
            mid_ref[x, 2 * side] = result[:, :LANES]
            mid_ref[x, 2 * side + 1] = result[:, LANES:]

        conv_rows(picks, mid_weight_ref, half_x + 2, put)
    weight = out_weight_ref[...]
    rows = (-1, 0, 1, TILE_Y - 2, TILE_Y - 1, TILE_Y)
    for x in range(TILE_X + 2):
        columns = []
        for y, k in zip(rows, (0, 1, 1, 2, 2, 3)):
            value = mid_ref[(x + 1) // 2, k]
            more = ()
            if x == 0:
                more += (x_lo,)
            if x == TILE_X + 1:
                more += (x_hi,)
            if y < 0:
                more += (y_lo,)
            if y == TILE_Y:
                more += (y_hi,)
            if more:
                columns.append(masked(value, *more))
            else:
                fine = act_ref[x - 1, y].astype(F32)
                columns.append((fine + value.astype(F32)).astype(BF))
        put_taps(weight, taps, [(x, k) for k in range(6)], columns)

    def received(ref, place, row):
        piece = ref[place].astype(F32)[row : row + 6]
        return piece[0:3] + piece[3:6]

    for x in range(TILE_X):
        for y in range(TILE_Y):
            near = [(a, b) for a in range(3) for b in range(3) if y + b - 1 in rows]
            starts = [(x + a, rows.index(y + b - 1), (a * 3 + b) * 24) for a, b in near]
            pieces = [taps[u, v, i : i + 24, :] for u, v, i in starts]
            if 0 < y < TILE_Y - 1:
                pieces.append(share_ref[x, y - 1])
            value = joined(added(pieces))
            x_ref = xl_ref if x == 0 else xh_ref
            y_ref = yl_ref if y == 0 else yh_ref
            on_x = x in (0, TILE_X - 1)
            on_y = y in (0, TILE_Y - 1)
            if on_x:
                value += received(x_ref, 8, y * 6)
            if on_y:
                value += received(y_ref, 12, x * 6)
            if on_x and on_y:
                value += received(y_ref, 12, 24 if x == 0 else 30)
            for d in range(3):
                field_ref[d, x * TILE_Y + y : x * TILE_Y + y + 1, :] = value[d : d + 1]
    sent_ref[...] = field_ref[...].astype(BF)


def gather_kernel(
    counts_ref, block_ref, dest_ref, own_ref, row_ref, y_two_ref, y_one_ref,
    nodes_ref, weight_ref, out_ref, frame, total,
):
    entries = weight_ref.shape[0]
    blocks = out_ref.shape[0]
    odd = (lax.axis_index("gy") + 1) % 2 == 1
    frame[5] = own_ref[...]
    for i in range(3):
        one = y_one_ref[i].astype(F32)
        two = y_two_ref[i].astype(F32)
        frame[3 * i + 1] = jnp.where(odd, one, two)
        frame[3 * i + 3] = jnp.where(odd, two, one)
        if i != 1:
            frame[3 * i + 2] = row_ref[i].astype(F32)
    total[...] = jnp.zeros(total.shape, F32)
    sub = lax.broadcasted_iota(I32, (8, LANES), 0)
    for e in range(entries):
        tile = dest_ref[e]
        d = (tile // lax.axis_size("gy") - lax.axis_index("gx") + 1) * 3 + (tile % lax.axis_size("gy") - lax.axis_index("gy") + 1)
        node = jnp.broadcast_to(nodes_ref[e : e + 1, :], (8, LANES))
        z = node & (LANES - 1)
        column = node >> 7
        rows = []
        for c in range(3):
            picked = None
            for q in range(4):
                table = frame[d + 1, c, q * 8 : q * 8 + 8, :]
                value = jnp.take_along_axis(table, z, axis=1)
                value = jnp.where(column == sub + q * 8, value, 0.0)
                picked = value if picked is None else picked + value
            rows.append(picked)
        wide = jnp.concatenate(rows, axis=0)
        high = wide.astype(BF)
        low = (wide - high.astype(F32)).astype(BF)
        both = jnp.concatenate([high, low], axis=0)
        value = lax.dot_general(both, weight_ref[e], NT, preferred_element_type=F32)
        block = block_ref[e]
        total[block] += value[0:24] + value[24:48]
    lane = lax.broadcasted_iota(I32, (1, LANES), 1)
    for b in range(blocks):
        live = lane < counts_ref[b]
        for c in range(3):
            value = jnp.sum(total[b, c * 8 : c * 8 + 8, :], axis=0, keepdims=True)
            out_ref[b, c : c + 1, :] = jnp.where(live, value, 0.0)


def partners(size_x, size_y, step_x, step_y, parity):
    left = [(0, y) for y in range(size_y)]
    top = [(x, size_y - 1) for x in range(1, size_x)]
    right = [(size_x - 1, y) for y in reversed(range(size_y - 1))]
    bottom = [(x, 0) for x in reversed(range(1, size_x - 1))]
    rim = left + top + right + bottom
    if not step_x:
        rim = rim[size_y - 1 :] + rim[: size_y - 1]
    partner = {}
    for x in range(size_x):
        for y in range(size_y):
            sign = 1 if (x if step_x else y) % 2 == parity else -1
            to = (x + sign * step_x, y + sign * step_y)
            if 0 <= to[0] < size_x and 0 <= to[1] < size_y:
                partner[x, y] = to
    alone = [place for place in rim if place not in partner]
    for one, two in zip(alone[::2], alone[1::2]):
        partner[one] = two
        partner[two] = one
    return partner


def swapped(value, step_x, step_y, parity):
    size_x = lax.axis_size("gx")
    size_y = lax.axis_size("gy")
    partner = partners(size_x, size_y, step_x, step_y, parity)
    pairs = [
        (x * size_y + y, to_x * size_y + to_y) for (x, y), (to_x, to_y) in sorted(partner.items())
    ]
    return lax.ppermute(value, ("gx", "gy"), pairs)


def across_x(one, two):
    return swapped(one, 1, 0, 1), swapped(two, 1, 0, 0)


def across_y(one, two):
    return swapped(one, 0, 1, 1), swapped(two, 0, 1, 0)


def shards(
    particle_feat, block_counts, entry_block, entry_dest, entry_nodes, entry_weights,
    conv_in, conv_mid, conv_out, head_weight,
):
    blocks = particle_feat.shape[0]
    entries = entry_weights.shape[0]
    dest = entry_dest.reshape(entries)
    in_weight = conv_in.reshape(3 * CHAN, 9 * CHAN)
    mid_weight = conv_mid.reshape(3 * CHAN, 9 * CHAN)
    folded = jnp.einsum(
        "do,aox->adx", head_weight, conv_out.astype(F32), precision=lax.Precision.HIGHEST
    )
    high = lax.reduce_precision(folded, 8, 7)
    both = jnp.concatenate([high, folded - high, jnp.zeros((3, 2, 9 * CHAN), F32)], axis=1)
    out_weight = (
        both.reshape(3, 8, 9, CHAN).transpose(0, 2, 1, 3).reshape(27 * 8, CHAN).astype(BF)
    )
    out_weight = jnp.pad(out_weight, ((0, PADDED - 27 * 8), (0, 0)))

    packed = (SLOTS * CHAN + 16, LANES)
    sent = call(
        partial_kernel,
        [(packed, BF)] * 9,
        [SM] * 3 + [HB, VM, HB],
        [
            pltpu.VMEM(particle_feat.shape, BF),
            pltpu.VMEM(entry_weights.shape, BF),
            pltpu.SemaphoreType.DMA((CHUNKS + 10,)),
            pltpu.VMEM((9, *packed), BF),
            pltpu.VMEM((entries, LANES), F32),
            pltpu.VMEM((entries, LANES), F32),
            pltpu.VMEM((9 * 16, LANES), F32),
            pltpu.SMEM((9,), I32),
        ],
        70000000,
        limit=60 * 1024 * 1024,
        to=HB,
    )(block_counts, entry_block, dest, particle_feat, entry_nodes, entry_weights)
    sides = [*across_x(sent[1], sent[2]), *across_y(sent[3], sent[4])]
    sums = scatter([sent[0]], None)[0]
    corners = sent[5:]
    corners = [
        swapped(value, 1, 1 - 2 * (i // 2), 1 - i % 2) for i, value in enumerate(corners)
    ]
    sums = scatter([*sides, *corners[:2]], sums)[0]
    outer, one, two = scatter(corners[2:], sums, OUTER)
    middle = scatter(corners[2:], sums, MIDDLE)[0]

    column = (CHAN, LANES)
    one, two = across_x(one, two)
    xl, xh, one, two = call(
        grid_side_kernel,
        [((TILE_Y, *column), BF)] * 2 + [((TILE_X + 2, *column), BF)] * 2,
        [VM] * 4,
        [pltpu.VMEM((TILE_X + 2, *column), BF)] * 2,
        1000000,
    )(one, two, outer, middle)
    one, two = across_y(one, two)
    stack, inner = call(
        inner_conv_kernel,
        [
            ((TILE_X + 2, TILE_Y, 3 * CHAN, LANES), BF),
            ((TILE_X, TILE_Y - 2, CHAN, LANES), BF),
        ],
        [VM] * 5,
        [],
        1000000000,
    )(outer, middle, xl, xh, in_weight)
    act, coarse, one, two = call(
        outer_conv_kernel,
        [
            ((TILE_X, TILE_Y, *column), BF),
            ((TILE_X // 2, TILE_Y // 2, *column), BF),
            ((9, *column), BF),
            ((9, *column), BF),
        ],
        [VM] * 8,
        [
            pltpu.VMEM((TILE_X + 2, 2, 3 * CHAN, LANES), BF),
            pltpu.VMEM((2, TILE_Y, 80, LANES), F32),
            pltpu.VMEM((9, *column), BF),
            pltpu.VMEM((9, *column), BF),
        ],
        600000000,
    )(outer, middle, stack, inner, one, two, in_weight, out_weight)

    one, two = across_x(one, two)
    down, up = call(
        rim_kernel,
        [((24, LANES), F32)] * 2,
        [VM] * 2,
        [pltpu.VMEM((TILE_X, PADDED, LANES), F32)],
        1000000000,
    )(act, out_weight)
    xl, xh, one, two = call(
        coarse_side_kernel,
        [((9, *column), BF)] * 2 + [((13, *column), BF)] * 2,
        [VM] * 5,
        [pltpu.VMEM((13, *column), BF)] * 2,
        1000000,
    )(one, two, coarse, down, up)
    one, two = across_y(one, two)
    stack, inner = call(
        inner_mid_kernel,
        [
            ((6, TILE_Y // 2, 3 * CHAN, LANES), BF),
            ((TILE_X, TILE_Y - 2, 24, LANES), F32),
        ],
        [VM] * 6,
        [pltpu.VMEM((TILE_X + 2, 4, PADDED, LANES), F32), pltpu.VMEM((4, 2, *column), BF)],
        1000000000,
    )(coarse, xl, xh, act, mid_weight, out_weight)
    field, rounded = call(
        outer_mid_kernel,
        [((3, TILE_X * TILE_Y, LANES), F32), ((3, TILE_X * TILE_Y, LANES), BF)],
        [VM] * 9,
        [
            pltpu.VMEM((6, 4, 3 * CHAN, LANES), BF),
            pltpu.VMEM((4, 4, *column), BF),
            pltpu.VMEM((TILE_X + 2, 6, PADDED, LANES), F32),
            pltpu.VMEM((13, *column), BF),
            pltpu.VMEM((13, *column), BF),
        ],
        1300000000,
    )(act, stack, inner, xl, xh, one, two, mid_weight, out_weight)

    one, two = across_x(rounded, rounded)
    row = call(
        field_side_kernel,
        [((3, 3, TILE_X * TILE_Y, LANES), BF)],
        [VM] * 3,
        [],
        1000000,
    )(one, two, rounded)[0]
    one, two = across_y(row, row)
    return call(
        gather_kernel,
        [((blocks, 3, LANES), F32)],
        [SM] * 3 + [VM] * 6,
        [
            pltpu.VMEM((10, 3, TILE_X * TILE_Y, LANES), F32),
            pltpu.VMEM((blocks, 24, LANES), F32),
        ],
        70000000,
    )(
        block_counts, entry_block, dest, field, row, two, one, entry_nodes, entry_weights
    )[0]


def solution(mesh):
    in_specs = (
        P(("gx", "gy"), None, None),
        P(("gx", "gy")),
        P(("gx", "gy")),
        P(("gx", "gy"), None),
        P(("gx", "gy"), None),
        P(("gx", "gy"), None, None),
        P(),
        P(),
        P(),
        P(),
    )
    out_specs = P(("gx", "gy"), None, None)
    return jax.shard_map(shards, mesh=mesh, in_specs=in_specs, out_specs=out_specs, check_vma=False)
```
